32 devices in a mesh: ctx: 4 (over y, core), exp: 8 (over z, x).
Axes of the slice: x: 2, y: 2, z: 4, core: 2. Of those that a mesh axis runs over, the one named last changes fastest.
Arguments:
- hits: bfloat16 [4096, 2048], P(('ctx', 'exp')), may hold values from -6 to 6
- cotangent: bfloat16 [4096, 2048], P(('ctx', 'exp')), may hold values from -6 to 6
- combine: float32 [4096, 2], P(('ctx', 'exp')), may hold values from 0.1 to 1
- expert_ids: int32 [4096, 2], P(('ctx', 'exp')), may hold values from 0 to 7, all different within a row; in each aligned block of 128 rows (0 to 127, 128 to 255, ...) at most 48 rows name the same one
- gate_weight: bfloat16 [8, 2048, 768], P('exp'), may hold values from -0.125 to 0.125
- up_weight: bfloat16 [8, 2048, 768], P('exp'), may hold values from -0.125 to 0.125
- down_weight: bfloat16 [8, 2048, 768], P('exp'), may hold values from -0.21875 to 0.21875
Outputs:
- mixed: bfloat16 [4096, 2048], P(('ctx', 'exp'))
- input_grads: bfloat16 [4096, 2048], P(('ctx', 'exp'))
- combine_grads: float32 [4096, 2], P(('ctx', 'exp'))
- gate_grads: bfloat16 [8, 2048, 768], P('exp', 'ctx')
- up_grads: bfloat16 [8, 2048, 768], P('exp', 'ctx')
- down_grads: bfloat16 [8, 2048, 768], P('exp', 'ctx')
The draws below stay inside these ranges and needn't reach their ends.
Inputs may be any that keep to these rules, and one draw needn't show every extreme that they name: `expert_ids`: the two ids of a hit differ. Among the 128 hits of one device no expert is named more than 48 times, and in every draw some device names some expert exactly 48 times.
All inputs are finite; a program needn't handle non-finite values.
Results may differ from the reference program's by a relative error of at most 0.017.
Values may be sent and summed in bfloat16 or wider, within the bound.
No kernel may reach another device: no remote copies, remote signals or barrier semaphores. Data moves between devices by JAX's collectives and lax.ppermute only.
A program may use at most 128 MiB of HBM per device.

```python
import math
import jax
import jax.numpy as jnp
import numpy as np
from jax import lax

D = 2048
FF = 768
TOK_DEV = 128
EXPERTS = 8
CAP = 48
TOKENS = 4096
N_CTX = 4
N_EXP = 8


def levels(rng, extent, cuts, least, top_value):
    gain, own = 1.0, jax.random.fold_in(rng, 6)
    for dim, shards_of in cuts:
        heights = jnp.exp(jax.random.uniform(jax.random.fold_in(own, dim), (shards_of,), jnp.float32, least / len(cuts), top_value / len(cuts)))
        gain = gain * jnp.repeat(heights, extent[dim] // shards_of).reshape([-1 if axis == dim else 1 for axis in range(len(extent))])
    return gain


def routed_block(rng, own, number, rows, amount, top, most, slope):
    sequence = jax.random.permutation(rng, amount)
    heavy_load, common = shares(amount, rows * top, most, slope, True), shares(amount, rows * top, most, slope, False)
    places = jnp.arange(amount)

    def named(lengths, offset_by):
        used = int((lengths > 0).sum())
        fixed = max(1, used // 4)
        moved = fixed + (places - fixed + offset_by * (used - fixed)) % max(1, amount - fixed)
        return jnp.zeros((amount,), jnp.int32).at[sequence[jnp.where(places < fixed, places, moved)]].set(jnp.asarray(lengths, jnp.int32))

    lengths = jnp.where(number % 4 == 0, named(heavy_load, number // 4), named(common, number - number // 4 - 1))
    mixed = jax.random.permutation(jax.random.fold_in(own, 3), amount)
    donor, taker = mixed[0:amount // 2 * 2:2], mixed[1:amount // 2 * 2:2]
    slack = jnp.minimum(lengths[donor] - 1, most - lengths[taker]) // 2
    slack = jnp.where((donor == sequence[0]) | (taker == sequence[0]) | (lengths[taker] == 0), 0, jnp.maximum(slack, 0))
    moved = jax.random.randint(jax.random.fold_in(own, 4), (amount // 2,), 0, 1 << 20) % (slack + 1)
    lengths = lengths.at[donor].add(-moved).at[taker].add(moved)
    items = jnp.searchsorted(jnp.cumsum(lengths), jnp.arange(rows * top), side="right").astype(jnp.int32)
    table = items.reshape(top, rows).T
    table = table[jax.random.permutation(jax.random.fold_in(own, 1), rows)]
    offset_by = jax.random.randint(jax.random.fold_in(own, 2), (rows, 1), 0, top)
    return jnp.take_along_axis(table, (jnp.arange(top)[None, :] + offset_by) % top, axis=1)


def shares(number_of, total, limit, slope, full):
    loads = [(1 << 20) // math.isqrt(rank ** slope) + 1 for rank in range(1, number_of + 1)]
    largest = limit if full else min(limit, max(-(-total // number_of), total * loads[0] // sum(loads)))
    least = 1 if total - largest >= number_of - 1 else 0
    given, surplus = [largest] + [least] * (number_of - 1), total - largest - least * (number_of - 1)
    while surplus > 0:
        movable = [i for i in range(1, number_of) if given[i] < largest] or [i for i in range(1, number_of) if given[i] < limit]
        pool, left = sum([loads[i] for i in movable]), surplus
        for i in movable:
            addition = min(limit - given[i], max(1, left * loads[i] // pool), surplus)
            given[i] = given[i] + addition
            surplus = surplus - addition
    return np.array(given)


def gaussian(key, dims, deviation, limit, split=(), kind=jnp.bfloat16):
    values = jax.random.normal(key, dims, jnp.float32) * deviation
    if len(split) > 0:
        values = levels(key, dims, split, -0.22, 0.18) * values
    return jnp.clip(values, min=-limit, max=limit).astype(kind)


def setup_inputs(seed: int = 0) -> dict:
    arg_keys = jax.random.split(jax.random.key(seed), 8)
    hits = gaussian(arg_keys[0], (TOKENS, D), 1.0, 6.0, ((0, 32),))
    cotangent = gaussian(arg_keys[1], (TOKENS, D), 1.0, 6.0, ((0, 32),))
    combine = jnp.clip(0.1 + 0.9 * jax.random.uniform(arg_keys[2], (TOKENS, 2), jnp.float32) ** levels(arg_keys[2], (TOKENS, 2), ((0, 32),), -0.2, 0.2), 0.1, 1.0)
    expert_ids_keys = jax.random.split(jax.random.fold_in(arg_keys[3], 1), TOKENS // TOK_DEV)
    expert_ids_turns = jax.random.permutation(jax.random.fold_in(arg_keys[3], 3), TOKENS // TOK_DEV)
    expert_ids = jax.vmap(lambda own, number: routed_block(jax.random.fold_in(arg_keys[3], 2), own, number, TOK_DEV, EXPERTS, 2, CAP, 2))(expert_ids_keys, expert_ids_turns).reshape((TOKENS, 2))
    gate_weight = gaussian(arg_keys[4], (EXPERTS, D, FF), D ** -0.5, 0.125, ((0, 8),))
    up_weight = gaussian(arg_keys[5], (EXPERTS, D, FF), D ** -0.5, 0.125, ((0, 8),))
    down_weight = gaussian(arg_keys[6], (EXPERTS, D, FF), FF ** -0.5, 0.21875, ((0, 8),))
    return {"hits": hits, "cotangent": cotangent, "combine": combine, "expert_ids": expert_ids, "gate_weight": gate_weight, "up_weight": up_weight, "down_weight": down_weight}


grad_scale = 0.0625


def expert_pass(slot_hits, slot_cot, w_gate, w_up, w_down):
    contract_hidden = (((1,), (1,)), ((), ()))
    gate_value = jnp.dot(slot_hits, w_gate, preferred_element_type=jnp.float32)
    up_value = jnp.dot(slot_hits, w_up, preferred_element_type=jnp.float32)
    sigmoid_gate = jax.nn.sigmoid(gate_value)
    active = gate_value * sigmoid_gate
    hidden = (active * up_value).astype(jnp.bfloat16)
    outputs = lax.dot_general(hidden, w_down, contract_hidden, preferred_element_type=jnp.float32).astype(jnp.bfloat16)
    grad_hidden = jnp.dot(slot_cot, w_down, preferred_element_type=jnp.float32)
    grad_up = (grad_hidden * active).astype(jnp.bfloat16)
    grad_gate = (grad_hidden * up_value * sigmoid_gate * (1.0 + gate_value * (1.0 - sigmoid_gate))).astype(jnp.bfloat16)
    grad_input = lax.dot_general(grad_gate, w_gate, contract_hidden, preferred_element_type=jnp.float32)
    grad_input = grad_input + lax.dot_general(grad_up, w_up, contract_hidden, preferred_element_type=jnp.float32)
    return outputs, grad_input.astype(jnp.bfloat16), hidden, grad_gate, grad_up


def ctx_partials(left_rows, right_rows):
    left_block = left_rows.reshape(N_CTX, -1, left_rows.shape[1]).astype(jnp.float32)
    right_block = right_rows.reshape(N_CTX, -1, right_rows.shape[1]).astype(jnp.float32)
    block_terms = jnp.einsum("crd,crf->cdf", left_block, right_block)
    rounded = lax.optimization_barrier(block_terms.astype(jnp.bfloat16))
    summed = jnp.sum(rounded.astype(jnp.float32), axis=0)
    return (summed * grad_scale).astype(jnp.bfloat16)


def reference(hits, cotangent, combine, expert_ids, gate_weight, up_weight, down_weight):
    devices_all = N_CTX * N_EXP
    routed = expert_ids.reshape(devices_all, 2 * TOK_DEV)
    catalog = jnp.arange(EXPERTS, dtype=jnp.int32)
    one_hot = (routed[:, :, None] == catalog[None, None, :]).astype(jnp.int32)
    slot_rank = jnp.sum((jnp.cumsum(one_hot, axis=1) - one_hot) * one_hot, axis=2)
    device_index = jnp.arange(devices_all, dtype=jnp.int32)[:, None]
    position = routed * (devices_all * CAP) + device_index * CAP + slot_rank
    pair_count = 2 * TOKENS
    table = jnp.full((EXPERTS * devices_all * CAP,), pair_count, jnp.int32)
    table = table.at[position.reshape(-1)].set(jnp.arange(pair_count, dtype=jnp.int32))
    table = table.reshape(EXPERTS, devices_all * CAP)
    flat_combine = combine.reshape(-1)

    def per_expert(carry, inputs):
        out_pairs, grad_pairs = carry
        w_gate, w_up, w_down, pair_ids = inputs
        valid = pair_ids < pair_count
        safe_pairs = jnp.where(valid, pair_ids, 0).astype(jnp.int32)
        owners = safe_pairs // 2
        slot_hits = jnp.where(valid[:, None], hits[owners], jnp.zeros((), jnp.bfloat16))
        weights_here = jnp.where(valid, flat_combine[safe_pairs], jnp.zeros((), jnp.float32))
        slot_cot = (weights_here[:, None] * cotangent[owners].astype(jnp.float32)).astype(jnp.bfloat16)
        outputs, grad_input, hidden, grad_gate, grad_up = expert_pass(slot_hits, slot_cot, w_gate, w_up, w_down)
        out_pairs = out_pairs.at[pair_ids].set(outputs, mode="drop")
        grad_pairs = grad_pairs.at[pair_ids].set(grad_input, mode="drop")
        gate_part = ctx_partials(slot_hits, grad_gate)
        up_part = ctx_partials(slot_hits, grad_up)
        down_part = ctx_partials(slot_cot, hidden)
        return (out_pairs, grad_pairs), (gate_part, up_part, down_part)

    zero_pairs = jnp.zeros((pair_count, D), jnp.bfloat16)
    (out_pairs, grad_pairs), (gate_grads, up_grads, down_grads) = lax.scan(
        per_expert, (zero_pairs, zero_pairs), (gate_weight, up_weight, down_weight, table))
    expert_out = out_pairs.reshape(TOKENS, 2, D).astype(jnp.float32)
    mixed = jnp.sum(combine[:, :, None] * expert_out, axis=1).astype(jnp.bfloat16)
    combine_grads = jnp.sum(cotangent[:, None, :].astype(jnp.float32) * expert_out, axis=2)
    input_grads = jnp.sum(grad_pairs.reshape(TOKENS, 2, D).astype(jnp.float32), axis=1).astype(jnp.bfloat16)
    return (mixed, input_grads, combine_grads, gate_grads, up_grads, down_grads)
```

```python
import jax
import jax.numpy as jnp
from jax import lax
from jax.sharding import PartitionSpec as P

grad_scale = 0.0625
f32 = jnp.float32
bf16 = jnp.bfloat16


def dot(a, b, dims=((1,), (0,))):
    return lax.dot_general(a, b, (dims, ((), ())), preferred_element_type=f32)


def exchange(x, axis, bit):
    size = lax.axis_size(axis)
    return lax.ppermute(x, axis, [(i, i ^ bit) for i in range(size)])


def within_half(blocks):
    return [blocks[0]] + [exchange(blocks[s], "exp", s) for s in range(1, len(blocks))]


def slot_plan(meta, half_experts, capacity):
    tokens = meta.shape[1]
    named = meta[:2, None, :] == half_experts.astype(f32)[None, :, None]
    either = (named[0] | named[1]).astype(bf16)
    place = jnp.arange(tokens)
    earlier = (place[:, None] < place[None, :]).astype(bf16)
    rank = dot(either, earlier)
    here = rank[:, None, :] == jnp.arange(capacity, dtype=f32)[None, :, None]
    return [(named[k][:, None, :] & here).astype(bf16).reshape(-1, tokens) for k in range(2)]


def gate_parts(gate, up):
    s = jax.nn.sigmoid(gate)
    active = gate * s
    return active, up * s * (1.0 + gate * (1.0 - s))


def scatter_sum(left, right):
    rows, width = left.shape
    size = lax.axis_size("ctx")
    me = lax.axis_index("ctx")
    share = width // size
    cols = left.reshape(rows, size // 2, 2, share)
    low = me % 2
    send_cols = lax.dynamic_index_in_dim(cols, 1 - low, 2, keepdims=False).reshape(rows, width // 2)
    keep_cols = lax.dynamic_index_in_dim(cols, low, 2, keepdims=False).reshape(rows, width // 2)
    send = dot(send_cols, right, ((0,), (0,))).astype(bf16)
    got = exchange(send, "ctx", 1)
    total = dot(keep_cols, right, ((0,), (0,))) + got.astype(f32)
    bit = 2
    while bit < size:
        groups = total.shape[0] // share
        parts = total.reshape(groups // 2, 2, share, -1)
        side = (me // bit) % 2
        send = lax.dynamic_index_in_dim(parts, 1 - side, 1, keepdims=False).reshape(groups // 2 * share, -1)
        keep = lax.dynamic_index_in_dim(parts, side, 1, keepdims=False).reshape(groups // 2 * share, -1)
        total = keep + exchange(send.astype(bf16), "ctx", bit).astype(f32)
        bit *= 2
    return total


def local(hits, cotangent, combine, expert_ids, gate_weight, up_weight, down_weight):
    tokens, width = hits.shape
    experts = lax.axis_size("exp")
    half = experts // 2
    capacity = 3 * tokens // experts
    me = lax.axis_index("exp")
    place = me % half
    half_experts = me - place + (place ^ jnp.arange(half, dtype=jnp.int32))
    w_gate, w_up, w_down = gate_weight[0], up_weight[0], down_weight[0]

    meta = jnp.concatenate([expert_ids.T.astype(f32), combine.T], axis=0)
    far_meta = exchange(meta, "exp", half)
    far_hits = exchange(hits, "exp", half)
    far_cot = exchange(cotangent, "exp", half)

    def weights_of(plan, m):
        return jnp.sum(plan[0].astype(f32) * m[2][None, :] + plan[1].astype(f32) * m[3][None, :], axis=1)

    def hit_slots(plan, x):
        return dot(plan[0] + plan[1], x).astype(bf16)

    def cot_slots(plan, m, x):
        return (weights_of(plan, m)[:, None] * dot(plan[0] + plan[1], x)).astype(bf16)

    def blocks_of(x):
        return [x[s * capacity : (s + 1) * capacity] for s in range(half)]

    def sum_out(plan, m, rows, cot):
        mixed, grads = 0.0, []
        for k in range(2):
            pair = dot(plan[k], rows, ((0,), (0,)))
            mixed = mixed + m[2 + k][:, None] * pair
            grads.append(jnp.sum(cot.astype(f32) * pair, axis=1))
        return mixed, jnp.stack(grads)

    own_plan = slot_plan(meta, half_experts, capacity)
    far_plan = slot_plan(far_meta, half_experts, capacity)

    own_send = jnp.concatenate([hit_slots(own_plan, hits), cot_slots(own_plan, meta, cotangent)], axis=1)
    own_rows = jnp.concatenate(within_half(blocks_of(own_send)), axis=0)
    x0, c0 = own_rows[:, :width], own_rows[:, width:]
    x1 = jnp.concatenate(within_half(blocks_of(hit_slots(far_plan, far_hits))), axis=0)
    c1 = jnp.concatenate(within_half(blocks_of(cot_slots(far_plan, far_meta, far_cot))), axis=0)

    def forward(x):
        gate, up = dot(x, w_gate), dot(x, w_up)
        active, slope = gate_parts(gate, up)
        hidden = (active * up).astype(bf16)
        return dot(hidden, w_down, ((1,), (1,))).astype(bf16), hidden, active, slope

    def backward(c, active, slope):
        grad_hidden = dot(c, w_down)
        grad_up = (grad_hidden * active).astype(bf16)
        grad_gate = (grad_hidden * slope).astype(bf16)
        grad_input = dot(grad_gate, w_gate, ((1,), (1,))) + dot(grad_up, w_up, ((1,), (1,)))
        return grad_input.astype(bf16), grad_gate, grad_up

    out0, hidden0, active0, slope0 = forward(x0)
    gin0, gg0, gu0 = backward(c0, active0, slope0)
    out1, hidden1, active1, slope1 = forward(x1)
    gin1, gg1, gu1 = backward(c1, active1, slope1)

    back_out1 = jnp.concatenate(within_half(blocks_of(out1)), axis=0)
    far_mixed, far_cg = sum_out(far_plan, far_meta, back_out1, far_cot)
    got_mixed = exchange(far_mixed.astype(bf16), "exp", half)
    got_cg = exchange(far_cg, "exp", half)
    back_gin1 = jnp.concatenate(within_half(blocks_of(gin1)), axis=0)
    far_gin = dot(far_plan[0] + far_plan[1], back_gin1, ((0,), (0,)))
    got_gin = exchange(far_gin.astype(bf16), "exp", half)

    back0 = jnp.concatenate(within_half(blocks_of(jnp.concatenate([out0, gin0], axis=1))), axis=0)
    own_mixed, own_cg = sum_out(own_plan, meta, back0[:, :width], cotangent)
    own_gin = dot(own_plan[0] + own_plan[1], back0[:, width:], ((0,), (0,)))

    mixed = (own_mixed + got_mixed.astype(f32)).astype(bf16)
    input_grads = (own_gin + got_gin.astype(f32)).astype(bf16)
    combine_grads = (own_cg + got_cg).T

    x = jnp.concatenate([x0, x1], axis=0)
    c = jnp.concatenate([c0, c1], axis=0)
    cat = lambda a, b: jnp.concatenate([a, b], axis=0)
    out = []
    for left, right in ((c, cat(hidden0, hidden1)), (x, cat(gg0, gg1)), (x, cat(gu0, gu1))):
        out.append((scatter_sum(left, right) * grad_scale).astype(bf16)[None])
    down_grads, gate_grads, up_grads = out
    return (mixed, input_grads, combine_grads, gate_grads, up_grads, down_grads)


def solution(mesh):
    rows = P(("ctx", "exp"), None)
    weight = P("exp", None, None)
    grads = P("exp", "ctx", None)
    return jax.shard_map(
        local,
        mesh=mesh,
        in_specs=(rows, rows, rows, rows, weight, weight, weight),
        out_specs=(rows, rows, rows, grads, grads, grads),
        check_vma=False,
    )
```

```python
import functools

import jax
import jax.numpy as jnp
from jax import lax
from jax.experimental import pallas as pl
from jax.experimental.pallas import tpu as pltpu
from jax.sharding import PartitionSpec as P

grad_scale = 0.0625
f32 = jnp.float32
bf16 = jnp.bfloat16
VMEM = pl.BlockSpec(memory_space=pltpu.VMEM)


def dot(a, b, dims=((1,), (0,))):
    return lax.dot_general(a, b, (dims, ((), ())), preferred_element_type=f32)


def exchange(x, axis, bit):
    size = lax.axis_size(axis)
    return lax.ppermute(x, axis, [(i, i ^ bit) for i in range(size)])


def within_half(blocks):
    return [blocks[0]] + [exchange(blocks[s], "exp", s) for s in range(1, len(blocks))]


def in_hbm(arrays):
    return list(arrays)


def result(shape, dtype):
    return jax.ShapeDtypeStruct(tuple(shape), dtype)


def params(**kw):
    return pltpu.CompilerParams(vmem_limit_bytes=24 * 1024 * 1024, **kw)


def cost(flops, bytes_accessed):
    return pl.CostEstimate(flops=1, bytes_accessed=1, transcendentals=0)


def after(value, *earlier):
    return lax.optimization_barrier((value, earlier))[0]


class Blocks:
    def __init__(self, half, capacity):
        self.half, self.capacity = half, capacity
        self.split = capacity % 16 == 0
        self.count = half if self.split else 1
        self.rows = half * capacity
        self.height = self.rows // self.count

    def shapes(self, width):
        return [result((self.height, width), bf16)] * self.count

    def send(self, arrays):
        if self.split:
            return within_half(arrays)
        blocks = [arrays[0][s * self.capacity : (s + 1) * self.capacity] for s in range(self.half)]
        return [jnp.concatenate(within_half(blocks), axis=0)]


def join(refs, cols=slice(None)):
    parts = [r[:, cols] for r in refs]
    return parts[0] if len(parts) == 1 else jnp.concatenate(parts, axis=0)


def store(refs, cols, value):
    height = refs[0].shape[0]
    for i, r in enumerate(refs):
        r[:, cols] = value[i * height : (i + 1) * height].astype(r.dtype)


def slot_plan(rows, form):
    tokens = rows[0].shape[1]
    me = lax.axis_index("exp")
    place = me % form.half
    slot = lax.broadcasted_iota(jnp.int32, (form.rows, 1), 0)
    block = jnp.zeros_like(slot)
    for i in range(1, form.half):
        block = block + (slot >= i * form.capacity).astype(jnp.int32)
    expert = (me - place + (block ^ place)).astype(f32)
    rank_here = (slot - block * form.capacity).astype(f32)
    first = (rows[0] == expert).astype(f32)
    second = (rows[1] == expert).astype(f32)
    row = lax.broadcasted_iota(jnp.int32, (tokens, tokens), 0)
    col = lax.broadcasted_iota(jnp.int32, (tokens, tokens), 1)
    earlier = (row < col).astype(f32).astype(bf16)
    rank = dot((first + second).astype(bf16), earlier)
    here = (rank == rank_here).astype(f32)
    return first * here, second * here


def pack_meta(ids, combine):
    pieces = []
    rest = combine
    for _ in range(3):
        top = lax.reduce_precision(rest, 8, 7)
        pieces.append(top)
        rest = rest - top
    packed = jnp.concatenate([ids.astype(f32)] + pieces, axis=1)
    return jnp.pad(packed, ((0, 0), (0, 128 - packed.shape[1]))).astype(bf16)


def packed_columns(ref):
    x = ref[...].astype(f32)
    return [x[:, k : k + 1] for k in range(2)] + [
        x[:, 2 + k : 3 + k] + x[:, 4 + k : 5 + k] + x[:, 6 + k : 7 + k] for k in range(2)
    ]


def packed_rows(ref):
    x = jnp.transpose(ref[...].astype(f32))
    return [x[k : k + 1] for k in range(2)] + [x[2 + k : 3 + k] + x[4 + k : 5 + k] + x[6 + k : 7 + k] for k in range(2)]


def plain_rows(ids_ref, combine_ref):
    ids = ids_ref[...].astype(f32)
    return [ids[0:1], ids[1:2], combine_ref[0:1, :], combine_ref[1:2, :]]


def chunks(width, step=512):
    step = min(step, width)
    return [slice(i, i + step) for i in range(0, width, step)]


def gather_kernel(form, scaled, width, plain, *refs):
    meta, refs = (plain_rows(*refs[:2]), refs[2:]) if plain else (packed_rows(refs[0]), refs[1:])
    inputs, outs = refs[: len(scaled)], refs[len(scaled) :]
    first, second = slot_plan(meta, form)
    either = (first + second).astype(bf16)
    weight = jnp.sum(first * meta[2] + second * meta[3], axis=1, keepdims=True)
    offset = 0
    for x, by_weight in zip(inputs, scaled):
        for cols in chunks(width):
            rows = dot(either, x[:, cols])
            if by_weight:
                rows = rows * weight
            store(outs, slice(offset + cols.start, offset + cols.stop), rows)
        offset += width


def meta_specs(meta, width):
    if len(meta) == 2:
        return [pl.BlockSpec(m.shape, lambda i: (0, 0)) for m in meta]
    return [pl.BlockSpec((meta[0].shape[0], 128), lambda i: (0, width // 128))]


def whole_spec(shape):
    return pl.BlockSpec(shape, lambda i: (0, 0))


def gather(form, meta, arrays, scaled, width):
    tokens = arrays[0].shape[0]
    total = width * len(arrays)
    out = pl.pallas_call(
        functools.partial(gather_kernel, form, scaled, width, len(meta) == 2),
        grid=(1,),
        out_shape=form.shapes(total),
        in_specs=meta_specs(meta, width) + [whole_spec((tokens, width)) for _ in arrays],
        out_specs=[whole_spec((form.height, total))] * form.count,
        compiler_params=params(),
        cost_estimate=cost(2 * form.rows * tokens * total, 4 * form.rows * total),
        name="gather_slots",
    )(*meta, *in_hbm(arrays))
    return list(out)


def back_kernel(form, offsets, plain, more, *refs):
    count = form.count
    if plain:
        meta, weights = plain_rows(*refs[:2]), [refs[2][:, k : k + 1] for k in range(2)]
        refs = refs[3:]
    else:
        meta, weights = packed_rows(refs[0]), packed_columns(refs[0])[2:]
        refs = refs[1:]
    cot_ref, rows, refs = refs[0], refs[1 : 1 + count], refs[1 + count :]
    others, outs = (list(refs[:2]), list(refs[2:])) if more else ([], list(refs))
    plan = [p.astype(bf16) for p in slot_plan(meta, form)]
    out_at, grad_at = offsets
    width = cot_ref.shape[1]

    def put(i, cols, value):
        if more:
            value = value + others[i][:, cols].astype(f32)
        outs[i][:, cols] = value.astype(outs[i].dtype)

    def put_grad(cols, value):
        if more:
            value = value + others[1][:, cols].astype(f32)
        outs[-1][:, cols] = value.astype(bf16)

    def put_sums(sums):
        if more:
            tail = others[0][:, width:].astype(f32)
            for k in range(2):
                outs[1][:, k : k + 1] = sums[k] + tail[:, k : k + 1] + tail[:, 2 + k : 3 + k] + tail[:, 4 + k : 5 + k]
            return
        lane = lax.broadcasted_iota(jnp.int32, (sums[0].shape[0], 128), 1)
        tail = jnp.zeros(lane.shape, f32)
        for k in range(2):
            rest = sums[k]
            for piece in range(3):
                top = rest.astype(bf16).astype(f32)
                tail = jnp.where(lane == 2 * piece + k, top, tail)
                rest = rest - top
        outs[0][:, width:] = tail.astype(bf16)

    if out_at is not None:
        sums = [0.0, 0.0]
        for cols in chunks(width):
            block = join(rows, slice(out_at + cols.start, out_at + cols.stop))
            mixed = 0.0
            cot = cot_ref[:, cols].astype(f32)
            for k in range(2):
                pair = dot(plan[k], block, ((0,), (0,)))
                mixed = mixed + weights[k] * pair
                sums[k] = sums[k] + jnp.sum(cot * pair, axis=1, keepdims=True)
            put(0, cols, mixed)
        put_sums(sums)
    if grad_at is not None:
        either = plan[0] + plan[1]
        for cols in chunks(width):
            block = join(rows, slice(grad_at + cols.start, grad_at + cols.stop))
            put_grad(cols, dot(either, block, ((0,), (0,))))


def back(form, meta, cot, rows, offsets, combine=None, others=()):
    tokens, width = cot.shape
    shapes = []
    if offsets[0] is not None:
        shapes += [result((tokens, width + (0 if others else 128)), bf16)]
    if others:
        shapes += [result((tokens, 2), f32)]
    if offsets[1] is not None:
        shapes += [result((tokens, width), bf16)]
    own = [] if combine is None else [combine]
    arrays = own + [cot] + list(rows) + list(others)
    return pl.pallas_call(
        functools.partial(back_kernel, form, offsets, combine is not None, len(others) > 0),
        grid=(1,),
        out_shape=shapes,
        in_specs=meta_specs(meta, width) + [whole_spec(a.shape) for a in arrays],
        out_specs=[whole_spec(x.shape) for x in shapes],
        compiler_params=params(),
        cost_estimate=cost(4 * form.rows * tokens * width, 4 * form.rows * width),
        name="sum_slots",
    )(*meta, *in_hbm(arrays))


def load_kernel(*refs):
    number = len(refs) // 2
    sems = refs[-1]
    copies = [pltpu.make_async_copy(refs[i].at[0], refs[number + i], sems.at[i]) for i in range(number)]
    for c in copies:
        c.start()
    for c in copies:
        c.wait()


def load(arrays):
    return pl.pallas_call(
        load_kernel,
        out_shape=[pltpu.VMEM(a.shape[1:], a.dtype) for a in arrays],
        in_specs=[pl.BlockSpec(memory_space=pl.ANY)] * len(arrays),
        out_specs=[VMEM] * len(arrays),
        scratch_shapes=[pltpu.SemaphoreType.DMA((len(arrays),))],
        compiler_params=params(),
        cost_estimate=cost(1, 1),
        name="load_weights",
    )(*arrays)


def in_vmem(arrays):
    return [pltpu.with_memory_space_constraint(a, pltpu.VMEM) for a in arrays]


def tiles(ff):
    return chunks(ff, 256 if ff % 256 == 0 else ff)


def add_to(acc, first, cols, value):
    if first:
        acc[:, cols] = value
    else:
        acc[:, cols] += value


def forward_kernel(count, *refs):
    x_refs, (gate_ref, up_ref, down_ref) = refs[:count], refs[count : count + 3]
    out_refs = refs[count + 3 : 2 * count + 3]
    hidden_ref, active_ref, slope_ref, acc = refs[2 * count + 3 :]
    x = join(x_refs)
    for step, inner in enumerate(tiles(hidden_ref.shape[1])):
        gate, up = dot(x, gate_ref[:, inner]), dot(x, up_ref[:, inner])
        s = jax.nn.sigmoid(gate)
        active = gate * s
        hidden = (active * up).astype(bf16)
        hidden_ref[:, inner] = hidden
        active_ref[:, inner] = active
        slope_ref[:, inner] = up * s * (1.0 + gate * (1.0 - s))
        for cols in chunks(acc.shape[1]):
            add_to(acc, step == 0, cols, dot(hidden, down_ref[cols, inner], ((1,), (1,))))
    store(out_refs, slice(None), acc[...])


def expert_call(kernel, form, inputs, weights, more, out_width, inner_types, name):
    width, ff = weights[0].shape
    rows = form.rows
    out_shape = form.shapes(out_width) + [jax.ShapeDtypeStruct((rows, ff), t) for t in inner_types]
    operands = [*inputs, *more]
    out = pl.pallas_call(
        functools.partial(kernel, form.count),
        out_shape=out_shape,
        in_specs=[VMEM] * (len(operands) + 3),
        out_specs=[VMEM] * len(out_shape),
        scratch_shapes=[pltpu.VMEM((rows, out_width), f32)],
        compiler_params=params(),
        cost_estimate=cost(6 * rows * width * ff, 6 * width * ff),
        name=name,
    )(*operands, *in_vmem(weights))
    return list(out[: form.count]), *out[form.count :]


def forward(form, x, *weights):
    return expert_call(forward_kernel, form, x, weights, [], weights[0].shape[0], [bf16, f32, f32], "expert_forward")


def backward_kernel(count, *refs):
    c_refs, (active_ref, slope_ref, gate_ref, up_ref, down_ref) = refs[:count], refs[count : count + 5]
    in_refs = refs[count + 5 : 2 * count + 5]
    gg_ref, gu_ref, acc = refs[2 * count + 5 :]
    c = join(c_refs)
    for step, inner in enumerate(tiles(gg_ref.shape[1])):
        grad_hidden = dot(c, down_ref[:, inner])
        gu = (grad_hidden * active_ref[:, inner]).astype(bf16)
        gg = (grad_hidden * slope_ref[:, inner]).astype(bf16)
        gu_ref[:, inner] = gu
        gg_ref[:, inner] = gg
        for cols in chunks(acc.shape[1]):
            back = dot(gg, gate_ref[cols, inner], ((1,), (1,))) + dot(gu, up_ref[cols, inner], ((1,), (1,)))
            add_to(acc, step == 0, cols, back)
    store(in_refs, slice(None), acc[...])


def backward(form, c, active, slope, *weights):
    more = [active, slope]
    return expert_call(backward_kernel, form, c, weights, more, weights[0].shape[0], [bf16, bf16], "expert_backward")


def both_kernel(count, *refs):
    in_refs, (gate_ref, up_ref, down_ref) = refs[:count], refs[count : count + 3]
    out_refs = refs[count + 3 : 2 * count + 3]
    hidden_ref, gg_ref, gu_ref, acc = refs[2 * count + 3 :]
    width = acc.shape[1] // 2
    x, c = join(in_refs, slice(0, width)), join(in_refs, slice(width, 2 * width))
    for step, inner in enumerate(tiles(hidden_ref.shape[1])):
        gate, up = dot(x, gate_ref[:, inner]), dot(x, up_ref[:, inner])
        s = jax.nn.sigmoid(gate)
        active = gate * s
        hidden = (active * up).astype(bf16)
        hidden_ref[:, inner] = hidden
        grad_hidden = dot(c, down_ref[:, inner])
        gu = (grad_hidden * active).astype(bf16)
        gg = (grad_hidden * up * s * (1.0 + gate * (1.0 - s))).astype(bf16)
        gu_ref[:, inner] = gu
        gg_ref[:, inner] = gg
        for cols in chunks(width):
            add_to(acc, step == 0, cols, dot(hidden, down_ref[cols, inner], ((1,), (1,))))
            back = slice(width + cols.start, width + cols.stop)
            grad = dot(gg, gate_ref[cols, inner], ((1,), (1,))) + dot(gu, up_ref[cols, inner], ((1,), (1,)))
            add_to(acc, step == 0, back, grad)
    store(out_refs, slice(None), acc[...])


def both(form, rows_in, *weights):
    return expert_call(both_kernel, form, rows_in, weights, [], 2 * weights[0].shape[0], [bf16] * 3, "expert_both")


def weight_kernel(counts, grads, adds, scale, beside, ids_ref, *refs):
    lefts = []
    for n in counts:
        lefts.append(join(refs[:n]))
        refs = refs[n:]
    number = 1 if beside else len(grads)
    outs, refs = refs[-number:], refs[:-number]
    if beside:
        ff = outs[0].shape[1] // len(grads)
        outs = [outs[0].at[:, i * ff : (i + 1) * ff] for i in range(len(grads))]
    rights, others = refs[: len(refs) - adds * len(grads)], refs[len(refs) - adds * len(grads) :]
    for i, (left, right) in enumerate(grads):
        rows = jnp.concatenate([rights[2 * right][...], rights[2 * right + 1][...]], axis=0)
        sums = dot(lefts[left], rows, ((0,), (0,)))
        for j in range(adds):
            sums = sums + others[j * len(grads) + i][...].astype(f32)
        if scale:
            sums = sums * grad_scale
        outs[i][...] = sums.astype(outs[i].dtype)


def weight_sums(form, ids, lefts, grads, share, adds=(), scale=False, dtype=bf16, beside=False):
    ff = grads[0][1][0].shape[1]
    steps = ids.shape[0]
    arrays, specs, counts = [], [], []
    for parts in lefts:
        counts.append(sum(len(p[0]) for p in parts))
        for held, part in parts:
            shares = held[0].shape[1] // share
            if part is None:
                part, blocks = 0, shares
            else:
                blocks = shares // 2
            arrays += held
            specs += [
                pl.BlockSpec((form.height, share), lambda i, ids_ref, at=part * blocks: (0, at + ids_ref[i]))
            ] * len(held)
    for _, pair in grads:
        arrays += pair
        specs += [pl.BlockSpec((form.rows, ff), lambda i, ids_ref: (0, 0))] * 2
    step = pl.BlockSpec((share, ff), lambda i, ids_ref: (i, 0))
    for group in adds:
        for array, column in group:
            arrays.append(array)
            specs.append(pl.BlockSpec((share, ff), lambda i, ids_ref, column=column: (i, column)))
    if beside:
        out_shape = [result((steps * share, len(grads) * ff), dtype)]
        out_specs = [pl.BlockSpec((share, len(grads) * ff), lambda i, ids_ref: (i, 0))]
    else:
        out_shape = [result((steps * share, ff), dtype)] * len(grads)
        out_specs = [step] * len(grads)
    return pl.pallas_call(
        functools.partial(weight_kernel, counts, [(g[0], i) for i, g in enumerate(grads)], len(adds), scale, beside),
        grid_spec=pltpu.PrefetchScalarGridSpec(
            num_scalar_prefetch=1, grid=(steps,), in_specs=specs, out_specs=out_specs
        ),
        out_shape=out_shape,
        compiler_params=params(),
        cost_estimate=cost(4 * form.rows * steps * share * ff, 4 * steps * share * ff),
        name="weight_sums",
    )(ids, *in_hbm(arrays))


def local(hits, cotangent, combine, expert_ids, gate_weight, up_weight, down_weight):
    tokens, width = hits.shape
    experts = lax.axis_size("exp")
    copies = lax.axis_size("ctx")
    half = experts // 2
    capacity = 3 * tokens // experts
    form = Blocks(half, capacity)
    far_hits = exchange(jnp.concatenate([hits, pack_meta(expert_ids, combine)], axis=1), "exp", half)
    far_cot = exchange(after(cotangent, far_hits), "exp", half)
    far_meta = (far_hits,)
    meta = (expert_ids.T, combine.T)

    weights = load([gate_weight, up_weight, down_weight])
    own_send = gather(form, after(meta, weights[0]), [hits, cotangent], (False, True), width)
    own = form.send(own_send)
    x1_sent = gather(form, after(far_meta, own_send[0]), [far_hits], (False,), width)
    x1 = form.send(x1_sent)
    back0, hidden0, gg0, gu0 = both(form, after(own, x1_sent[0]), *weights)
    out1, hidden1, active1, slope1 = forward(form, after(x1, hidden0), *weights)
    out1_back = form.send(out1)
    c1_sent = gather(form, after(far_meta, hidden1), [far_cot], (True,), width)
    c1 = form.send(c1_sent)
    (far_mixed,) = back(form, after(far_meta, c1_sent[0]), far_cot, out1_back, (0, None))
    got_mixed = exchange(far_mixed, "exp", half)

    share = width // copies
    order = [r for r in range(0, copies, 2)]
    order.sort(key=lambda r: [-(r >> b & 1) for b in range(1, copies.bit_length())])
    order = jnp.asarray(order, jnp.int32)
    here = lax.axis_index("ctx")
    on = copies // 4
    theirs, ours = here ^ 1 ^ order, here ^ order
    x_rows, c_rows = [(own, 0), (x1, None)], [(own, 1), (c1, None)]
    down = [(0, (hidden0, hidden1))]

    (down_low,) = weight_sums(form, after(theirs[:on], far_mixed, c1), [c_rows], down, share)
    down_got = exchange(down_low, "ctx", 1)
    back0_got = form.send(after(back0, down_low))
    (down_on,) = weight_sums(form, ours[:on], [c_rows], down, share, [[(down_got, 0)]])
    pad = jnp.zeros((share // 8, down_on.shape[1]), bf16)
    down_there = exchange(jnp.concatenate([down_on, pad], axis=0), "ctx", 2)
    gin1, gg1, gu1 = backward(form, after(c1, down_on), active1, slope1, *weights)
    gin1_back = form.send(gin1)
    gate, up = [(0, (gg0, gg1))], [(0, (gu0, gu1))]
    (gate_low,) = weight_sums(form, theirs[:on], [x_rows], gate, share)
    gate_got = exchange(gate_low, "ctx", 1)
    (down_low,) = weight_sums(form, after(theirs[on:], gate_low), [c_rows], down, share)
    down_got = exchange(down_low, "ctx", 1)
    (up_low,) = weight_sums(form, after(theirs[:on], down_low, back0_got, got_mixed), [x_rows], up, share)
    up_got = exchange(up_low, "ctx", 1)
    (both_on,) = weight_sums(
        form,
        after(ours[:on], up_low, down_there, down_got),
        [x_rows],
        gate + up,
        share,
        [[(gate_got, 0), (up_got, 0)]],
        beside=True,
    )
    both_there = exchange(both_on, "ctx", 2)
    (far_grad,) = back(form, after(far_meta, both_on), far_cot, gin1_back, (None, 0))
    got_grad = exchange(far_grad, "exp", half)

    last = copies == 4
    kind = dict(scale=last, dtype=bf16 if last else f32)

    def stay(sums):
        bit = 4
        while bit < copies:
            middle = sums.shape[0] // 2
            sums = sums[middle:] + exchange(sums[:middle].astype(bf16), "ctx", bit).astype(f32)
            bit *= 2
        return (sums if last else (sums * grad_scale).astype(bf16))[None]

    lows = weight_sums(form, after(theirs[on:], far_grad), [x_rows], gate + up, share)
    gate_got, up_got = [exchange(low, "ctx", 1) for low in lows]
    (down_sums,) = weight_sums(
        form, after(ours[on:], lows[0]), [c_rows], down, share, [[(down_got, 0)], [(down_there, 0)]], **kind
    )
    mixed, combine_grads, input_grads = back(
        form, after(meta, down_sums, gate_got, up_got), cotangent, back0_got, (0, width), combine, (got_mixed, got_grad)
    )
    gate_sums, up_sums = weight_sums(
        form,
        after(ours[on:], mixed),
        [x_rows],
        gate + up,
        share,
        [[(gate_got, 0), (up_got, 0)], [(both_there, 0), (both_there, 1)]],
        **kind,
    )
    return (mixed, input_grads, combine_grads, stay(gate_sums), stay(up_sums), stay(down_sums))


def solution(mesh):
    rows = P(("ctx", "exp"), None)
    weight = P("exp", None, None)
    grads = P("exp", "ctx", None)
    return jax.shard_map(
        local,
        mesh=mesh,
        in_specs=(rows, rows, rows, rows, weight, weight, weight),
        out_specs=(rows, rows, rows, grads, grads, grads),
        check_vma=False,
    )
```

```python
import functools

import jax
import jax.numpy as jnp
from jax import lax
from jax.experimental import pallas as pl
from jax.experimental.pallas import tpu as pltpu
from jax.sharding import PartitionSpec as P

grad_scale = 0.0625
f32 = jnp.float32
bf16 = jnp.bfloat16
VMEM = pl.BlockSpec(memory_space=pltpu.VMEM)
SMEM = pl.BlockSpec(memory_space=pltpu.SMEM)


def dot(a, b, dims=((1,), (0,))):
    return lax.dot_general(a, b, (dims, ((), ())), preferred_element_type=f32)


def exchange(x, axis, bit):
    size = lax.axis_size(axis)
    return lax.ppermute(x, axis, [(i, i ^ bit) for i in range(size)])


def within_half(blocks):
    return [blocks[0]] + [exchange(blocks[s], "exp", s) for s in range(1, len(blocks))]


def in_hbm(arrays):
    return [pltpu.with_memory_space_constraint(a, pltpu.HBM) for a in arrays]


def result(shape, dtype):
    return jax.ShapeDtypeStruct(tuple(shape), dtype)


def params(**kw):
    return pltpu.CompilerParams(vmem_limit_bytes=24 * 1024 * 1024, **kw)


def cost(flops, bytes_accessed):
    return pl.CostEstimate(flops=1, bytes_accessed=1, transcendentals=0)


def after(value, *earlier):
    return lax.optimization_barrier((value, earlier))[0]


class Blocks:
    def __init__(self, half, capacity):
        self.half, self.capacity = half, capacity
        self.split = capacity % 16 == 0
        self.count = half if self.split else 1
        self.rows = half * capacity
        self.height = self.rows // self.count

    def shapes(self, width):
        return [result((self.height, width), bf16)] * self.count

    def send(self, arrays, early=None):
        if self.split:
            if early is not None:
                number, first, then = early
                arrays = after(arrays[:number], first) + after(arrays[number:], then)
            return within_half(arrays)
        blocks = [arrays[0][s * self.capacity : (s + 1) * self.capacity] for s in range(self.half)]
        return [jnp.concatenate(within_half(blocks), axis=0)]


def join(refs, cols=slice(None)):
    parts = [r[:, cols] for r in refs]
    return parts[0] if len(parts) == 1 else jnp.concatenate(parts, axis=0)


def store(refs, cols, value):
    height = refs[0].shape[0]
    for i, r in enumerate(refs):
        r[:, cols] = value[i * height : (i + 1) * height].astype(r.dtype)


def slot_plan(rows, form):
    tokens = rows[0].shape[1]
    me = lax.axis_index("exp")
    place = me % form.half
    slot = lax.broadcasted_iota(jnp.int32, (form.rows, 1), 0)
    block = jnp.zeros_like(slot)
    for i in range(1, form.half):
        block = block + (slot >= i * form.capacity).astype(jnp.int32)
    expert = (me - place + (block ^ place)).astype(f32)
    rank_here = (slot - block * form.capacity).astype(f32)
    first = (rows[0] == expert).astype(f32)
    second = (rows[1] == expert).astype(f32)
    row = lax.broadcasted_iota(jnp.int32, (tokens, tokens), 0)
    col = lax.broadcasted_iota(jnp.int32, (tokens, tokens), 1)
    earlier = (row < col).astype(f32).astype(bf16)
    rank = dot((first + second).astype(bf16), earlier)
    here = (rank == rank_here).astype(f32)
    return first * here, second * here


def packed_columns(ref):
    x = ref[...].astype(f32)
    return [x[:, k : k + 1] for k in range(2)] + [
        x[:, 2 + k : 3 + k] + x[:, 4 + k : 5 + k] + x[:, 6 + k : 7 + k] for k in range(2)
    ]


def packed_rows(ref):
    x = jnp.transpose(ref[...].astype(f32))
    return [x[k : k + 1] for k in range(2)] + [x[2 + k : 3 + k] + x[4 + k : 5 + k] + x[6 + k : 7 + k] for k in range(2)]


def plain_rows(ids_ref, combine_ref):
    ids = ids_ref[...].astype(f32)
    return [ids[0:1], ids[1:2], combine_ref[0:1, :], combine_ref[1:2, :]]


def chunks(width, step=512):
    step = min(step, width)
    return [slice(i, i + step) for i in range(0, width, step)]


def pack_rows(meta):
    rows = [meta[0], meta[1]]
    rest = [meta[2], meta[3]]
    for _ in range(3):
        top = [r.astype(bf16).astype(f32) for r in rest]
        rows += top
        rest = [r - t for r, t in zip(rest, top)]
    rows.append(jnp.zeros((128 - len(rows), meta[0].shape[1]), f32))
    return jnp.transpose(jnp.concatenate(rows, axis=0)).astype(bf16)


def gather_kernel(form, scaled, width, plain, *refs):
    meta, refs = (plain_rows(*refs[:2]), refs[2:]) if plain else (packed_rows(refs[0]), refs[1:])
    if plain:
        message_ref, refs = refs[-1], refs[:-1]
        message_ref[:, :width] = refs[0][...]
        message_ref[:, width:] = pack_rows(meta)
    inputs, outs = refs[: len(scaled)], refs[len(scaled) :]
    first, second = slot_plan(meta, form)
    either = (first + second).astype(bf16)
    weight = jnp.sum(first * meta[2] + second * meta[3], axis=1, keepdims=True)
    offset = 0
    for x, by_weight in zip(inputs, scaled):
        for cols in chunks(width):
            rows = dot(either, x[:, cols])
            if by_weight:
                rows = rows * weight
            store(outs, slice(offset + cols.start, offset + cols.stop), rows)
        offset += width


def meta_specs(meta, width):
    if len(meta) == 2:
        return [pl.BlockSpec(m.shape, lambda i: (0, 0)) for m in meta]
    return [pl.BlockSpec((meta[0].shape[0], 128), lambda i: (0, width // 128))]


def whole_spec(shape):
    return pl.BlockSpec(shape, lambda i: (0, 0))


def gather(form, meta, arrays, scaled, width):
    tokens = arrays[0].shape[0]
    total = width * len(arrays)
    plain = len(meta) == 2
    out_shape = form.shapes(total)
    if plain:
        out_shape = out_shape + [result((tokens, width + 128), bf16)]
    out = pl.pallas_call(
        functools.partial(gather_kernel, form, scaled, width, plain),
        grid=(1,),
        out_shape=out_shape,
        in_specs=meta_specs(meta, width) + [whole_spec((tokens, width)) for _ in arrays],
        out_specs=[whole_spec(x.shape) for x in out_shape],
        compiler_params=params(),
        cost_estimate=cost(2 * form.rows * tokens * total, 4 * form.rows * total),
        name="gather_slots",
    )(*(in_hbm([*meta, *arrays]) if plain else [*meta, *arrays]))
    return list(out)


def back_kernel(form, offsets, plain, more, *refs):
    count = form.count
    if plain:
        meta, weights = plain_rows(*refs[:2]), [refs[2][:, k : k + 1] for k in range(2)]
        refs = refs[3:]
    else:
        meta, weights = packed_rows(refs[0]), packed_columns(refs[0])[2:]
        refs = refs[1:]
    cot_ref, rows, refs = refs[0], refs[1 : 1 + count], refs[1 + count :]
    others, outs = (list(refs[:2]), list(refs[2:])) if more else ([], list(refs))
    plan = [p.astype(bf16) for p in slot_plan(meta, form)]
    out_at, grad_at = offsets
    width = cot_ref.shape[1]

    def put(i, cols, value):
        if more:
            value = value + others[i][:, cols].astype(f32)
        outs[i][:, cols] = value.astype(outs[i].dtype)

    def put_grad(cols, value):
        if more:
            value = value + others[1][:, cols].astype(f32)
        outs[-1][:, cols] = value.astype(bf16)

    def put_sums(sums):
        if more:
            tail = others[0][:, width:].astype(f32)
            for k in range(2):
                outs[1][:, k : k + 1] = sums[k] + tail[:, k : k + 1] + tail[:, 2 + k : 3 + k] + tail[:, 4 + k : 5 + k]
            return
        lane = lax.broadcasted_iota(jnp.int32, (sums[0].shape[0], 128), 1)
        tail = jnp.zeros(lane.shape, f32)
        for k in range(2):
            rest = sums[k]
            for piece in range(3):
                top = rest.astype(bf16).astype(f32)
                tail = jnp.where(lane == 2 * piece + k, top, tail)
                rest = rest - top
        outs[0][:, width:] = tail.astype(bf16)

    if out_at is not None:
        sums = [0.0, 0.0]
        for cols in chunks(width):
            block = join(rows, slice(out_at + cols.start, out_at + cols.stop))
            mixed = 0.0
            cot = cot_ref[:, cols].astype(f32)
            for k in range(2):
                pair = dot(plan[k], block, ((0,), (0,)))
                mixed = mixed + weights[k] * pair
                sums[k] = sums[k] + jnp.sum(cot * pair, axis=1, keepdims=True)
            put(0, cols, mixed)
        put_sums(sums)
    if grad_at is not None:
        either = plan[0] + plan[1]
        for cols in chunks(width):
            block = join(rows, slice(grad_at + cols.start, grad_at + cols.stop))
            put_grad(cols, dot(either, block, ((0,), (0,))))


def back(form, meta, cot, rows, offsets, combine=None, others=()):
    tokens, width = cot.shape
    shapes = []
    if offsets[0] is not None:
        shapes += [result((tokens, width + (0 if others else 128)), bf16)]
    if others:
        shapes += [result((tokens, 2), f32)]
    if offsets[1] is not None:
        shapes += [result((tokens, width), bf16)]
    own = [] if combine is None else [combine]
    arrays = own + [cot] + list(rows) + list(others)
    return pl.pallas_call(
        functools.partial(back_kernel, form, offsets, combine is not None, len(others) > 0),
        grid=(1,),
        out_shape=shapes,
        in_specs=meta_specs(meta, width) + [whole_spec(a.shape) for a in arrays],
        out_specs=[whole_spec(x.shape) for x in shapes],
        compiler_params=params(),
        cost_estimate=cost(4 * form.rows * tokens * width, 4 * form.rows * width),
        name="sum_slots",
    )(*meta, *arrays)


def tiles(ff):
    return chunks(ff, 256 if ff % 256 == 0 else ff)


def fetch(refs, buffers, sems, steps):
    copies = [
        [
            pltpu.make_async_copy(w.at[0, :, inner], b.at[:, inner], sems.at[i, step])
            for i, (w, b) in enumerate(zip(refs, buffers))
        ]
        for step, inner in enumerate(steps)
    ]
    for group in copies:
        for c in group:
            c.start()

    def wait(step):
        for c in copies[step]:
            c.wait()

    return wait


def add_to(acc, first, cols, value):
    if first:
        acc[:, cols] = value
    else:
        acc[:, cols] += value


def pick(ids_ref, refs, at, out_ref, out_at, width):
    number = ids_ref.shape[0]
    share = width // (2 * number)
    height = refs[0].shape[0]
    for p in range(number):
        cols = pl.ds(pl.multiple_of(at + ids_ref[p] * share, share), share)
        for i, r in enumerate(refs):
            out_ref[i * height : (i + 1) * height, out_at + p * share : out_at + (p + 1) * share] = r[:, cols]
    return out_at + number * share


def pick_kernel(count, ids_ref, *refs):
    pick(ids_ref, refs[:count], 0, refs[count], 0, refs[0].shape[1])


def pick_shares(form, ids, arrays):
    width = arrays[0].shape[1]
    return pl.pallas_call(
        functools.partial(pick_kernel, form.count),
        out_shape=jax.ShapeDtypeStruct((form.rows, width // 2), bf16),
        in_specs=[SMEM] + [VMEM] * form.count,
        out_specs=VMEM,
        compiler_params=params(),
        cost_estimate=cost(1, 1),
        name="pick_shares",
    )(ids, *arrays)


def forward_kernel(count, *refs):
    x_refs, ids_ref, held = refs[:count], refs[count], refs[count + 1 : count + 4]
    out_refs = refs[count + 4 : 2 * count + 4]
    swap_ref, hidden_ref, active_ref, slope_ref, acc, gate_ref, up_ref, down_ref, sems = refs[2 * count + 4 :]
    wait = fetch(held, (gate_ref, up_ref, down_ref), sems, tiles(hidden_ref.shape[1]))
    x = join(x_refs)
    ff = hidden_ref.shape[1]
    used = pick(ids_ref, x_refs, 0, swap_ref, 0, x.shape[1])
    for step, inner in enumerate(tiles(hidden_ref.shape[1])):
        wait(step)
        gate, up = dot(x, gate_ref[:, inner]), dot(x, up_ref[:, inner])
        s = jax.nn.sigmoid(gate)
        active = gate * s
        hidden = (active * up).astype(bf16)
        hidden_ref[:, inner] = hidden
        swap_ref[:, used + inner.start : used + inner.stop] = hidden
        active_ref[:, inner] = active
        slope_ref[:, inner] = up * s * (1.0 + gate * (1.0 - s))
        for cols in chunks(acc.shape[1]):
            add_to(acc, step == 0, cols, dot(hidden, down_ref[cols, inner], ((1,), (1,))))
    store(out_refs, slice(None), acc[...])


def expert_call(kernel, form, inputs, weights, more, out_width, inner_types, name):
    _, width, ff = weights[0].shape
    rows = form.rows
    out_shape = form.shapes(out_width) + [jax.ShapeDtypeStruct((rows, w), t) for w, t in inner_types]
    operands = [*inputs, *more]
    out = pl.pallas_call(
        functools.partial(kernel, form.count),
        out_shape=out_shape,
        in_specs=[SMEM if o.dtype == jnp.int32 else VMEM for o in operands] + [pl.BlockSpec(memory_space=pl.ANY)] * 3,
        out_specs=[VMEM] * len(out_shape),
        scratch_shapes=[pltpu.VMEM((rows, out_width), f32)]
        + [pltpu.VMEM((width, ff), bf16)] * 3
        + [pltpu.SemaphoreType.DMA((3, len(tiles(ff))))],
        compiler_params=params(),
        cost_estimate=cost(6 * rows * width * ff, 6 * width * ff),
        name=name,
    )(*operands, *in_hbm(weights))
    return list(out[: form.count]), *out[form.count :]


def forward(form, x, ids, *weights):
    _, width, ff = weights[0].shape
    types = [(width // 2 + ff, bf16), (ff, bf16), (ff, f32), (ff, f32)]
    return expert_call(forward_kernel, form, x, weights, [ids], width, types, "expert_forward")


def backward_kernel(count, *refs):
    c_refs, active_ref, slope_ref, held = refs[:count], refs[count], refs[count + 1], refs[count + 2 : count + 5]
    in_refs = refs[count + 5 : 2 * count + 5]
    gg_ref, gu_ref, acc, gate_ref, up_ref, down_ref, sems = refs[2 * count + 5 :]
    wait = fetch(held, (gate_ref, up_ref, down_ref), sems, tiles(gg_ref.shape[1]))
    c = join(c_refs)
    for step, inner in enumerate(tiles(gg_ref.shape[1])):
        wait(step)
        grad_hidden = dot(c, down_ref[:, inner])
        gu = (grad_hidden * active_ref[:, inner]).astype(bf16)
        gg = (grad_hidden * slope_ref[:, inner]).astype(bf16)
        gu_ref[:, inner] = gu
        gg_ref[:, inner] = gg
        for cols in chunks(acc.shape[1]):
            back = dot(gg, gate_ref[cols, inner], ((1,), (1,))) + dot(gu, up_ref[cols, inner], ((1,), (1,)))
            add_to(acc, step == 0, cols, back)
    store(in_refs, slice(None), acc[...])


def backward(form, c, active, slope, *weights):
    more = [active, slope]
    _, width, ff = weights[0].shape
    return expert_call(backward_kernel, form, c, weights, more, width, [(ff, bf16)] * 2, "expert_backward")


def both_kernel(count, *refs):
    in_refs, ids_ref, held = refs[:count], refs[count], refs[count + 1 : count + 4]
    out_refs = refs[count + 4 : 2 * count + 4]
    picked_ref, inner_ref, acc, gate_ref, up_ref, down_ref, sems = refs[2 * count + 4 :]
    width, ff = acc.shape[1] // 2, gate_ref.shape[1]
    wait = fetch(held, (gate_ref, up_ref, down_ref), sems, tiles(ff))
    used = pick(ids_ref, in_refs, 0, picked_ref, 0, width)
    pick(ids_ref, in_refs, width, picked_ref, used, width)
    hidden_ref, gg_ref, gu_ref = [inner_ref.at[:, i * ff : (i + 1) * ff] for i in range(3)]
    x, c = join(in_refs, slice(0, width)), join(in_refs, slice(width, 2 * width))
    for step, inner in enumerate(tiles(ff)):
        wait(step)
        gate, up = dot(x, gate_ref[:, inner]), dot(x, up_ref[:, inner])
        s = jax.nn.sigmoid(gate)
        active = gate * s
        hidden = (active * up).astype(bf16)
        hidden_ref[:, inner] = hidden
        grad_hidden = dot(c, down_ref[:, inner])
        gu = (grad_hidden * active).astype(bf16)
        gg = (grad_hidden * up * s * (1.0 + gate * (1.0 - s))).astype(bf16)
        gu_ref[:, inner] = gu
        gg_ref[:, inner] = gg
        for cols in chunks(width):
            add_to(acc, step == 0, cols, dot(hidden, down_ref[cols, inner], ((1,), (1,))))
            back = slice(width + cols.start, width + cols.stop)
            grad = dot(gg, gate_ref[cols, inner], ((1,), (1,))) + dot(gu, up_ref[cols, inner], ((1,), (1,)))
            add_to(acc, step == 0, back, grad)
    store(out_refs, slice(None), acc[...])


def both(form, rows_in, ids, *weights):
    _, width, ff = weights[0].shape
    return expert_call(both_kernel, form, rows_in, weights, [ids], 2 * width, [(width, bf16), (3 * ff, bf16)], "expert_both")


def weight_kernel(counts, adds, scale, ids_ref, *refs):
    groups = []
    for n in counts:
        groups.append(join(refs[:n]))
        refs = refs[n:]
    left = jnp.concatenate(groups, axis=0)
    number = len(refs) // (len(counts) + adds + 1)
    rights, refs = refs[: number * len(counts)], refs[number * len(counts) :]
    others, outs = refs[:-number], refs[-number:]
    for i in range(number):
        right = jnp.concatenate([r[...] for r in rights[i * len(counts) : (i + 1) * len(counts)]], axis=0)
        sums = dot(left, right, ((0,), (0,)))
        if adds:
            sums = sums + others[i][...].astype(f32)
        if scale:
            sums = sums * grad_scale
        outs[i][...] = sums.astype(outs[i].dtype)


def weight_sums(form, ids, at, left, rights, share, ff, add=None, scale=False, dtype=bf16, hbm=False):
    first, steps = at[0], at[1] - at[0]
    arrays, specs = [], []
    for held, column, picked in left:
        block = column // share
        for h in held:
            arrays.append(h)
            if picked:
                specs.append(pl.BlockSpec((h.shape[0], share), lambda i, ids_ref, b=block: (0, b + first + i)))
            else:
                specs.append(pl.BlockSpec((h.shape[0], share), lambda i, ids_ref, b=block: (0, b + ids_ref[first + i])))
    for right in rights:
        for array, column in right:
            arrays.append(array)
            specs.append(pl.BlockSpec((form.rows, ff), lambda i, ids_ref, b=column // ff: (0, b)))
    for array, column in add or []:
        arrays.append(array)
        specs.append(pl.BlockSpec((share, ff), lambda i, ids_ref, b=column // ff: (i, b)))
    number = len(rights)
    widths = [ff] * number
    if hbm:
        arrays = in_hbm(arrays)
    return pl.pallas_call(
        functools.partial(weight_kernel, [len(g[0]) for g in left], 1 if add else 0, scale),
        grid_spec=pltpu.PrefetchScalarGridSpec(
            num_scalar_prefetch=1,
            grid=(steps,),
            in_specs=specs,
            out_specs=[pl.BlockSpec((share, w), lambda i, ids_ref: (i, 0)) for w in widths],
        ),
        out_shape=[jax.ShapeDtypeStruct((steps * share, w), dtype) for w in widths],
        compiler_params=params(),
        cost_estimate=cost(1, 1),
        name="weight_sums",
    )(ids, *arrays)


def finish_kernel(number, *refs):
    for keep, got, out in zip(refs[:number], refs[number : 2 * number], refs[2 * number :]):
        out[...] = ((keep[...] + got[...].astype(f32)) * grad_scale).astype(bf16)


def finish(keeps, gots):
    number = len(keeps)
    rows, ff = keeps[0].shape
    tile = rows // 2
    return pl.pallas_call(
        functools.partial(finish_kernel, number),
        grid=(rows // tile,),
        out_shape=[result((rows, ff), bf16)] * number,
        in_specs=[pl.BlockSpec((tile, ff), lambda i: (i, 0))] * (2 * number),
        out_specs=[pl.BlockSpec((tile, ff), lambda i: (i, 0))] * number,
        compiler_params=params(),
        cost_estimate=cost(1, 1),
        name="finish_weights",
    )(*keeps, *gots)


def local(hits, cotangent, combine, expert_ids, gate_weight, up_weight, down_weight):
    tokens, width = hits.shape
    experts = lax.axis_size("exp")
    copies = lax.axis_size("ctx")
    half = experts // 2
    capacity = 3 * tokens // experts
    form = Blocks(half, capacity)
    meta = (expert_ids.T, combine.T)
    *own_send, message = gather(form, meta, [hits, cotangent], (False, True), width)
    far_hits = exchange(message, "exp", half)
    far_cot = exchange(after(cotangent, far_hits), "exp", half)
    far_meta = (far_hits,)

    share, ff = width // copies, gate_weight.shape[2]
    order = [r for r in range(0, copies, 2)]
    order.sort(key=lambda r: [-(r >> b & 1) for b in range(1, copies.bit_length())])
    order = jnp.asarray(order, jnp.int32)
    here = lax.axis_index("ctx")
    theirs, ours = here ^ 1 ^ order, here ^ order
    swap = lambda x: exchange(x, "ctx", 1)

    weights = (gate_weight, up_weight, down_weight)
    own = form.send(own_send)
    x1_sent = gather(form, after(far_meta, own), [far_hits], (False,), width)
    x1 = form.send(x1_sent)
    back0, own_picked, own_inner = both(form, after(own, x1_sent[0]), theirs, *weights)
    picked_got, inner_got = swap(own_picked), swap(own_inner)
    c1_sent = gather(form, after(far_meta, own_picked), [far_cot], (True,), width)
    c1 = form.send(c1_sent)
    out1, x1_swap, hidden1, active1, slope1 = forward(form, after(x1, c1_sent[0]), theirs, *weights)
    x1_got = swap(x1_swap)
    out1_back = form.send(out1)

    on, all_ = copies // 4, copies // 2
    half_width = width // 2
    c1_got = swap(pick_shares(form, after(theirs, hidden1), c1))
    x_left = [(own, 0, False), (x1, 0, False), ([picked_got], 0, True), ([x1_got], 0, True)]
    c_left = [(own, width, False), (c1, 0, False), ([picked_got], half_width, True), ([c1_got], 0, True)]
    at_hidden, at_gate, at_up = [i * ff for i in range(3)]

    def right(far, far_got, column, far_column=0):
        return [(own_inner, column), (far, 0), (inner_got, column), (far_got, far_column)]

    hidden1_got = x1_got[:, half_width:]
    down = [right(hidden1, hidden1_got, at_hidden)]
    (down_on,) = weight_sums(form, ours, (0, on), c_left, down, share, ff)
    down_there = exchange(down_on, "ctx", 2)
    gin1, gg1, gu1 = backward(form, after(c1, down_on), active1, slope1, *weights)
    gin1_back = form.send(gin1)
    (far_mixed,) = back(form, after(far_meta, gg1), far_cot, out1_back, (0, None))
    got_mixed = exchange(far_mixed, "exp", half)
    both_rights = [right(gg1, swap(gg1), at_gate), right(gu1, swap(gu1), at_up)]
    gate_on, up_on = weight_sums(form, after(ours, far_mixed), (0, on), x_left, both_rights, share, ff)
    gate_there, up_there = exchange(gate_on, "ctx", 2), exchange(up_on, "ctx", 2)
    (far_grad,) = back(form, after(far_meta, gate_on, down_there), far_cot, gin1_back, (None, 0))
    got_grad = exchange(far_grad, "exp", half)

    def last_bits(keep, got):
        bit = 4
        while bit < copies:
            sums = keep + got.astype(f32)
            middle = sums.shape[0] // 2
            keep, got = sums[middle:], exchange(sums[:middle].astype(bf16), "ctx", bit)
            bit *= 2
        return keep, got

    back0_got = form.send(back0, (2, down_on, far_grad))
    (down_keep,) = weight_sums(form, after(ours, far_grad, got_mixed, back0_got[1 % form.count]), (on, all_), c_left, down, share, ff, dtype=f32, hbm=True)
    gate_keep, up_keep = weight_sums(
        form, after(ours, down_keep), (on, all_), x_left, both_rights, share, ff, dtype=f32, hbm=True
    )
    mixed, combine_grads, input_grads = back(
        form,
        after(meta, gate_keep),
        cotangent,
        back0_got,
        (0, width),
        combine,
        (got_mixed, got_grad),
    )
    down_grads, gate_grads, up_grads = [
        finish([k for k, _ in pairs], [g for _, g in pairs])
        for pairs in [[last_bits(down_keep, down_there)]]
    ][0] + finish(*zip(*[last_bits(gate_keep, gate_there), last_bits(up_keep, up_there)]))
    return (mixed, input_grads, combine_grads, gate_grads[None], up_grads[None], down_grads[None])


def solution(mesh):
    rows = P(("ctx", "exp"), None)
    weight = P("exp", None, None)
    grads = P("exp", "ctx", None)
    return jax.shard_map(
        local,
        mesh=mesh,
        in_specs=(rows, rows, rows, rows, weight, weight, weight),
        out_specs=(rows, rows, rows, grads, grads, grads),
        check_vma=False,
    )
```

```python
import functools

import jax
import jax.numpy as jnp
from jax import lax
from jax.experimental import pallas as pl
from jax.experimental.pallas import tpu as pltpu
from jax.sharding import PartitionSpec as P

grad_scale = 0.0625
f32 = jnp.float32
bf16 = jnp.bfloat16
VMEM = pl.BlockSpec(memory_space=pltpu.VMEM)
SMEM = pl.BlockSpec(memory_space=pltpu.SMEM)


def dot(a, b, dims=((1,), (0,))):
    return lax.dot_general(a, b, (dims, ((), ())), preferred_element_type=f32)


def exchange(x, axis, bit):
    size = lax.axis_size(axis)
    return lax.ppermute(x, axis, [(i, i ^ bit) for i in range(size)])


def within_half(blocks, places=None):
    places = range(len(blocks)) if places is None else places
    return [exchange(blocks[s], "exp", s) if s else blocks[0] for s in places]


def in_hbm(arrays):
    return [pltpu.with_memory_space_constraint(a, pltpu.HBM) for a in arrays]


def result(shape, dtype):
    return jax.ShapeDtypeStruct(tuple(shape), dtype)


def params(**kw):
    return pltpu.CompilerParams(vmem_limit_bytes=24 * 1024 * 1024, **kw)


def cost(weight):
    return pl.CostEstimate(flops=1 + int(weight * 7.5e9), bytes_accessed=1, transcendentals=0)


def after(value, *earlier):
    return lax.optimization_barrier((value, earlier))[0]


class Blocks:
    def __init__(self, half, capacity):
        self.half, self.capacity = half, capacity
        self.split = capacity % 16 == 0
        self.count = half if self.split else 1
        self.rows = half * capacity
        self.height = self.rows // self.count

    def shapes(self, width):
        return [result((self.height, width), bf16)] * self.count

    def send(self, arrays, places=None):
        if self.split:
            return within_half(arrays, places)
        blocks = [arrays[0][s * self.capacity : (s + 1) * self.capacity] for s in range(self.half)]
        return [jnp.concatenate(within_half(blocks), axis=0)]


def join(refs, cols=slice(None)):
    parts = [r[:, cols] for r in refs]
    return parts[0] if len(parts) == 1 else jnp.concatenate(parts, axis=0)


def turned(blocks):
    return list(blocks[:1]) + list(blocks[1:])[::-1]


def store(refs, cols, value):
    height = refs[0].shape[0]
    for i, r in enumerate(refs):
        r[:, cols] = value[i * height : (i + 1) * height].astype(r.dtype)


def slot_plan(rows, form):
    tokens = rows[0].shape[1]
    me = lax.axis_index("exp")
    place = me % form.half
    slot = lax.broadcasted_iota(jnp.int32, (form.rows, 1), 0)
    block = jnp.zeros_like(slot)
    for i in range(1, form.half):
        block = block + (slot >= i * form.capacity).astype(jnp.int32)
    expert = (me - place + (block ^ place)).astype(f32)
    rank_here = (slot - block * form.capacity).astype(f32)
    first = (rows[0] == expert).astype(f32)
    second = (rows[1] == expert).astype(f32)
    row = lax.broadcasted_iota(jnp.int32, (tokens, tokens), 0)
    col = lax.broadcasted_iota(jnp.int32, (tokens, tokens), 1)
    earlier = (row < col).astype(f32).astype(bf16)
    rank = dot((first + second).astype(bf16), earlier)
    here = (rank == rank_here).astype(f32)
    return first * here, second * here


def packed_columns(ref):
    x = ref[...].astype(f32)
    return [x[:, k : k + 1] for k in range(2)] + [
        x[:, 2 + k : 3 + k] + x[:, 4 + k : 5 + k] + x[:, 6 + k : 7 + k] for k in range(2)
    ]


def packed_rows(ref):
    x = jnp.transpose(ref[...].astype(f32))
    return [x[k : k + 1] for k in range(2)] + [x[2 + k : 3 + k] + x[4 + k : 5 + k] + x[6 + k : 7 + k] for k in range(2)]


def plain_rows(ids_ref, combine_ref):
    ids = ids_ref[...].astype(f32)
    return [ids[0:1], ids[1:2], combine_ref[0:1, :], combine_ref[1:2, :]]


def chunks(width, step=512):
    step = min(step, width)
    return [slice(i, i + step) for i in range(0, width, step)]


def pack_rows(meta):
    rows = [meta[0], meta[1]]
    rest = [meta[2], meta[3]]
    for _ in range(3):
        top = [r.astype(bf16).astype(f32) for r in rest]
        rows += top
        rest = [r - t for r, t in zip(rest, top)]
    rows.append(jnp.zeros((128 - len(rows), meta[0].shape[1]), f32))
    return jnp.transpose(jnp.concatenate(rows, axis=0)).astype(bf16)


def gather_kernel(form, scaled, width, plain, *refs):
    meta, refs = (plain_rows(*refs[:2]), refs[2:]) if plain else (packed_rows(refs[0]), refs[1:])
    if plain:
        message_ref, refs = refs[-1], refs[:-1]
        message_ref[:, :width] = refs[0][...]
        message_ref[:, width:] = pack_rows(meta)
    inputs, outs = refs[: len(scaled)], refs[len(scaled) :]
    first, second = slot_plan(meta, form)
    either = (first + second).astype(bf16)
    weight = jnp.sum(first * meta[2] + second * meta[3], axis=1, keepdims=True)
    offset = 0
    for x, by_weight in zip(inputs, scaled):
        for cols in chunks(width):
            rows = dot(either, x[:, cols])
            if by_weight:
                rows = rows * weight
            store(outs, slice(offset + cols.start, offset + cols.stop), rows)
        offset += width


def meta_specs(meta, width):
    if len(meta) == 2:
        return [pl.BlockSpec(m.shape, lambda i: (0, 0)) for m in meta]
    return [pl.BlockSpec((meta[0].shape[0], 128), lambda i: (0, width // 128))]


def whole_spec(shape):
    return pl.BlockSpec(shape, lambda i: (0, 0))


def gather(form, meta, arrays, scaled, width, weight=0.0):
    tokens = arrays[0].shape[0]
    total = width * len(arrays)
    plain = len(meta) == 2
    out_shape = form.shapes(total)
    if plain:
        out_shape = out_shape + [result((tokens, width + 128), bf16)]
    out = pl.pallas_call(
        functools.partial(gather_kernel, form, scaled, width, plain),
        grid=(1,),
        out_shape=out_shape,
        in_specs=meta_specs(meta, width) + [whole_spec((tokens, width)) for _ in arrays],
        out_specs=[whole_spec(x.shape) for x in out_shape],
        compiler_params=params(),
        cost_estimate=cost(weight),
        name="gather_slots",
    )(*(in_hbm([*meta, *arrays]) if plain else [*meta, *arrays]))
    return list(out)


def back_kernel(form, offsets, plain, more, *refs):
    count = form.count
    if plain:
        meta, weights = plain_rows(*refs[:2]), [refs[2][:, k : k + 1] for k in range(2)]
        refs = refs[3:]
    else:
        meta, weights = packed_rows(refs[0]), packed_columns(refs[0])[2:]
        refs = refs[1:]
    cot_ref, rows, refs = refs[0], turned(refs[1 : 1 + count]), refs[1 + count :]
    others, outs = (list(refs[:1]), list(refs[1:])) if more else ([], list(refs))
    plan = [p.astype(bf16) for p in slot_plan(meta, form)]
    out_at, grad_at = offsets
    width = cot_ref.shape[1]

    def put(i, cols, value):
        if more:
            value = value + others[i][:, cols].astype(f32)
        outs[i][:, cols] = value.astype(outs[i].dtype)

    def put_grad(cols, value):
        outs[-1][:, cols] = value.astype(outs[-1].dtype)

    def put_sums(sums):
        lane = lax.broadcasted_iota(jnp.int32, (sums[0].shape[0], 128), 1)
        if more:
            tail = jnp.transpose(others[0][:, width:].astype(f32))
            rows = jnp.transpose(jnp.where(lane == 0, sums[0], jnp.where(lane == 1, sums[1], 0.0)))
            outs[1][...] = rows[0:2] + tail[0:2] + tail[2:4] + tail[4:6]
            return
        tail = jnp.zeros(lane.shape, f32)
        for k in range(2):
            rest = sums[k]
            for piece in range(3):
                top = rest.astype(bf16).astype(f32)
                tail = jnp.where(lane == 2 * piece + k, top, tail)
                rest = rest - top
        outs[0][:, width:] = tail.astype(bf16)

    if out_at is not None:
        sums = [0.0, 0.0]
        for cols in chunks(width):
            block = join(rows, slice(out_at + cols.start, out_at + cols.stop))
            mixed = 0.0
            cot = cot_ref[:, cols].astype(f32)
            for k in range(2):
                pair = dot(plan[k], block, ((0,), (0,)))
                mixed = mixed + weights[k] * pair
                sums[k] = sums[k] + jnp.sum(cot * pair, axis=1, keepdims=True)
            put(0, cols, mixed)
        put_sums(sums)
    if grad_at is not None:
        either = plan[0] + plan[1]
        for cols in chunks(width):
            block = join(rows, slice(grad_at + cols.start, grad_at + cols.stop))
            put_grad(cols, dot(either, block, ((0,), (0,))))


def back(form, meta, cot, rows, offsets, combine=None, others=(), weight=0.0):
    tokens, width = cot.shape
    shapes = []
    if offsets[0] is not None:
        shapes += [result((tokens, width + (0 if others else 128)), bf16)]
    if others:
        shapes += [result((2, tokens), f32)]
    if offsets[1] is not None:
        shapes += [jax.ShapeDtypeStruct((tokens, width), f32 if others else bf16)]
    own = [] if combine is None else [combine]
    arrays = own + [cot] + turned(rows) + list(others)
    return pl.pallas_call(
        functools.partial(back_kernel, form, offsets, combine is not None, len(others) > 0),
        grid=(1,),
        out_shape=shapes,
        in_specs=meta_specs(meta, width) + [whole_spec(a.shape) for a in arrays],
        out_specs=[whole_spec(x.shape) for x in shapes],
        compiler_params=params(),
        cost_estimate=cost(weight),
        name="sum_slots",
    )(*meta, *arrays)


def tiles(ff):
    return chunks(ff, 256 if ff % 256 == 0 else ff)


def fetch(refs, buffers, sems, steps):
    copies = [
        [
            pltpu.make_async_copy(w.at[0, :, inner], b.at[:, inner], sems.at[i, step])
            for i, (w, b) in enumerate(zip(refs, buffers))
        ]
        for step, inner in enumerate(steps)
    ]
    for group in copies:
        for c in group:
            c.start()

    def wait(step):
        for c in copies[step]:
            c.wait()

    return wait


def add_to(acc, first, cols, value):
    if first:
        acc[:, cols] = value
    else:
        acc[:, cols] += value


def pick(ids_ref, refs, at, out_ref, out_at, width):
    number = ids_ref.shape[0]
    share = width // (2 * number)
    height = refs[0].shape[0]
    for p in range(number):
        cols = pl.ds(pl.multiple_of(at + ids_ref[p] * share, share), share)
        for i, r in enumerate(refs):
            out_ref[i * height : (i + 1) * height, out_at + p * share : out_at + (p + 1) * share] = r[:, cols]
    return out_at + number * share


def pick_kernel(count, ids_ref, *refs):
    pick(ids_ref, turned(refs[:count]), 0, refs[count], 0, refs[0].shape[1])


def pick_shares(form, ids, arrays, weight=0.0):
    width = arrays[0].shape[1]
    return pl.pallas_call(
        functools.partial(pick_kernel, form.count),
        out_shape=jax.ShapeDtypeStruct((form.rows, width // 2), bf16),
        in_specs=[SMEM] + [VMEM] * form.count,
        out_specs=VMEM,
        compiler_params=params(),
        cost_estimate=cost(weight),
        name="pick_shares",
    )(ids, *turned(arrays))


def forward_kernel(count, *refs):
    x_refs, ids_ref, held = turned(refs[:count]), refs[count], refs[count + 1 : count + 4]
    out_refs = refs[count + 4 : 2 * count + 4]
    swap_ref, hidden_ref, active_ref, slope_ref, acc, gate_ref, up_ref, down_ref, sems = refs[2 * count + 4 :]
    wait = fetch(held, (gate_ref, up_ref, down_ref), sems, tiles(hidden_ref.shape[1]))
    x = join(x_refs)
    ff = hidden_ref.shape[1]
    used = pick(ids_ref, x_refs, 0, swap_ref, 0, x.shape[1])
    for step, inner in enumerate(tiles(hidden_ref.shape[1])):
        wait(step)
        gate, up = dot(x, gate_ref[:, inner]), dot(x, up_ref[:, inner])
        s = jax.nn.sigmoid(gate)
        active = gate * s
        hidden = (active * up).astype(bf16)
        hidden_ref[:, inner] = hidden
        swap_ref[:, used + inner.start : used + inner.stop] = hidden
        active_ref[:, inner] = active
        slope_ref[:, inner] = up * s * (1.0 + gate * (1.0 - s))
        for cols in chunks(acc.shape[1]):
            add_to(acc, step == 0, cols, dot(hidden, down_ref[cols, inner], ((1,), (1,))))
    store(out_refs, slice(None), acc[...])


def expert_call(kernel, form, inputs, weights, more, out_width, inner_types, name, weight=0.0):
    _, width, ff = weights[0].shape
    rows = form.rows
    out_shape = form.shapes(out_width) + [jax.ShapeDtypeStruct((rows, w), t) for w, t in inner_types]
    operands = [*turned(inputs), *more]
    out = pl.pallas_call(
        functools.partial(kernel, form.count),
        out_shape=out_shape,
        in_specs=[SMEM if o.dtype == jnp.int32 else VMEM for o in operands] + [pl.BlockSpec(memory_space=pl.ANY)] * 3,
        out_specs=[VMEM] * len(out_shape),
        scratch_shapes=[pltpu.VMEM((rows, out_width), f32)]
        + [pltpu.VMEM((width, ff), bf16)] * 3
        + [pltpu.SemaphoreType.DMA((3, len(tiles(ff))))],
        compiler_params=params(),
        cost_estimate=cost(weight),
        name=name,
    )(*operands, *in_hbm(weights))
    return list(out[: form.count]), *out[form.count :]


def forward(form, x, ids, *weights, weight=0.0):
    _, width, ff = weights[0].shape
    types = [(width // 2 + ff, bf16), (ff, bf16), (ff, f32), (ff, f32)]
    return expert_call(forward_kernel, form, x, weights, [ids], width, types, "expert_forward", weight)


def backward_kernel(count, *refs):
    c_refs, active_ref, slope_ref, held = turned(refs[:count]), refs[count], refs[count + 1], refs[count + 2 : count + 5]
    in_refs = refs[count + 5 : 2 * count + 5]
    gg_ref, gu_ref, acc, gate_ref, up_ref, down_ref, sems = refs[2 * count + 5 :]
    wait = fetch(held, (gate_ref, up_ref, down_ref), sems, tiles(gg_ref.shape[1]))
    c = join(c_refs)
    for step, inner in enumerate(tiles(gg_ref.shape[1])):
        wait(step)
        grad_hidden = dot(c, down_ref[:, inner])
        gu = (grad_hidden * active_ref[:, inner]).astype(bf16)
        gg = (grad_hidden * slope_ref[:, inner]).astype(bf16)
        gu_ref[:, inner] = gu
        gg_ref[:, inner] = gg
        for cols in chunks(acc.shape[1]):
            back = dot(gg, gate_ref[cols, inner], ((1,), (1,))) + dot(gu, up_ref[cols, inner], ((1,), (1,)))
            add_to(acc, step == 0, cols, back)
    store(in_refs, slice(None), acc[...])


def backward(form, c, active, slope, *weights, weight=0.0):
    more = [active, slope]
    _, width, ff = weights[0].shape
    return expert_call(backward_kernel, form, c, weights, more, width, [(ff, bf16)] * 2, "expert_backward", weight)


def both_kernel(count, *refs):
    in_refs, ids_ref, held = turned(refs[:count]), refs[count], refs[count + 1 : count + 4]
    out_refs = refs[count + 4 : 2 * count + 4]
    picked_ref, inner_ref, acc, gate_ref, up_ref, down_ref, sems = refs[2 * count + 4 :]
    width, ff = acc.shape[1] // 2, gate_ref.shape[1]
    wait = fetch(held, (gate_ref, up_ref, down_ref), sems, tiles(ff))
    used = pick(ids_ref, in_refs, 0, picked_ref, 0, width)
    pick(ids_ref, in_refs, width, picked_ref, used, width)
    hidden_ref, gg_ref, gu_ref = [inner_ref.at[:, i * ff : (i + 1) * ff] for i in range(3)]
    x, c = join(in_refs, slice(0, width)), join(in_refs, slice(width, 2 * width))
    for step, inner in enumerate(tiles(ff)):
        wait(step)
        gate, up = dot(x, gate_ref[:, inner]), dot(x, up_ref[:, inner])
        s = jax.nn.sigmoid(gate)
        active = gate * s
        hidden = (active * up).astype(bf16)
        hidden_ref[:, inner] = hidden
        grad_hidden = dot(c, down_ref[:, inner])
        gu = (grad_hidden * active).astype(bf16)
        gg = (grad_hidden * up * s * (1.0 + gate * (1.0 - s))).astype(bf16)
        gu_ref[:, inner] = gu
        gg_ref[:, inner] = gg
        for cols in chunks(width):
            add_to(acc, step == 0, cols, dot(hidden, down_ref[cols, inner], ((1,), (1,))))
            back = slice(width + cols.start, width + cols.stop)
            grad = dot(gg, gate_ref[cols, inner], ((1,), (1,))) + dot(gu, up_ref[cols, inner], ((1,), (1,)))
            add_to(acc, step == 0, back, grad)
    store(out_refs, slice(None), acc[...])


def both(form, rows_in, ids, *weights):
    _, width, ff = weights[0].shape
    return expert_call(both_kernel, form, rows_in, weights, [ids], 2 * width, [(width, bf16), (3 * ff, bf16)], "expert_both")


def weight_kernel(counts, number, ids_ref, *refs):
    groups = []
    for n in counts:
        groups.append(join(turned(refs[:n])))
        refs = refs[n:]
    left = jnp.concatenate(groups, axis=0)
    rights, outs = refs[: number * len(counts)], refs[number * len(counts) :]
    if len(outs) < number:
        ff = outs[0].shape[1] // number
        outs = [outs[0].at[:, i * ff : (i + 1) * ff] for i in range(number)]
    for i in range(number):
        right = jnp.concatenate([r[...] for r in rights[i * len(counts) : (i + 1) * len(counts)]], axis=0)
        outs[i][...] = dot(left, right, ((0,), (0,))).astype(outs[i].dtype)


def weight_sums(form, ids, at, left, rights, share, ff, dtype=bf16, hbm=False, beside=False, weight=0.0):
    first, steps = at[0], at[1] - at[0]
    arrays, specs = [], []
    for held, column, picked in left:
        block = column // share
        for h in turned(held):
            arrays.append(h)
            if picked:
                specs.append(pl.BlockSpec((h.shape[0], share), lambda i, ids_ref, b=block: (0, b + first + i)))
            else:
                specs.append(pl.BlockSpec((h.shape[0], share), lambda i, ids_ref, b=block: (0, b + ids_ref[first + i])))
    for right in rights:
        for array, column in right:
            arrays.append(array)
            specs.append(pl.BlockSpec((form.rows, ff), lambda i, ids_ref, b=column // ff: (0, b)))
    number = len(rights)
    widths = [number * ff] if beside else [ff] * number
    if hbm:
        arrays = in_hbm(arrays)
    return pl.pallas_call(
        functools.partial(weight_kernel, [len(g[0]) for g in left], number),
        grid_spec=pltpu.PrefetchScalarGridSpec(
            num_scalar_prefetch=1,
            grid=(steps,),
            in_specs=specs,
            out_specs=[pl.BlockSpec((share, w), lambda i, ids_ref: (i, 0)) for w in widths],
        ),
        out_shape=[jax.ShapeDtypeStruct((steps * share, w), dtype) for w in widths],
        compiler_params=params(),
        cost_estimate=cost(weight),
        name="weight_sums",
    )(ids, *arrays)


def add_kernel(a_ref, b_ref, out_ref):
    out_ref[...] = (a_ref[...] + b_ref[...].astype(f32)).astype(bf16)


def add_up(a, b):
    rows, width = a.shape
    block = pl.BlockSpec((rows, width // 2), lambda i: (0, i))
    return pl.pallas_call(
        add_kernel,
        grid=(2,),
        out_shape=result((rows, width), bf16),
        in_specs=[block] * 2,
        out_specs=block,
        compiler_params=params(),
        cost_estimate=cost(0),
        name="add_halves",
    )(a, b)


def finish_kernel(number, *refs):
    for keep, got, out in zip(refs[:number], refs[number : 2 * number], refs[2 * number :]):
        out[...] = ((keep[...] + got[...].astype(f32)) * grad_scale).astype(bf16)


def finish(keep, got, number, weight=0.0):
    rows, ff = keep.shape[0], keep.shape[1] // number
    tile = rows // 2
    sides = [pl.BlockSpec((tile, ff), lambda i, n=n: (i, n)) for n in range(number)]
    return pl.pallas_call(
        functools.partial(finish_kernel, number),
        grid=(rows // tile,),
        out_shape=[result((rows, ff), bf16)] * number,
        in_specs=sides * 2,
        out_specs=[pl.BlockSpec((tile, ff), lambda i: (i, 0))] * number,
        compiler_params=params(),
        cost_estimate=cost(weight),
        name="finish_weights",
    )(*[keep] * number, *[got] * number)


def local(hits, cotangent, combine, expert_ids, gate_weight, up_weight, down_weight):
    tokens, width = hits.shape
    experts = lax.axis_size("exp")
    copies = lax.axis_size("ctx")
    half = experts // 2
    capacity = 3 * tokens // experts
    form = Blocks(half, capacity)
    meta = (expert_ids.T, combine.T)
    *own_send, message = gather(form, meta, [hits, cotangent], (False, True), width)
    far_hits = exchange(message, "exp", half)
    far_cot = exchange(after(cotangent, far_hits), "exp", half)
    far_meta = (far_hits,)

    share, ff = width // copies, gate_weight.shape[2]
    order = [r for r in range(0, copies, 2)]
    order.sort(key=lambda r: [-(r >> b & 1) for b in range(1, copies.bit_length())])
    order = jnp.asarray(order, jnp.int32)
    here = lax.axis_index("ctx")
    theirs, ours = here ^ 1 ^ order, here ^ order
    swap = lambda x: exchange(x, "ctx", 1)

    weights = (gate_weight, up_weight, down_weight)
    own = form.send(own_send)
    x1_sent = gather(form, after(far_meta, own), [far_hits], (False,), width)
    x1 = form.send(x1_sent)
    back0, own_picked, own_inner = both(form, after(own, x1_sent[0]), theirs, *weights)
    picked_got, inner_got = swap(own_picked), swap(own_inner)
    c1_sent = gather(form, after(far_meta, own_picked), [far_cot], (True,), width)
    c1 = form.send(c1_sent)
    out1, x1_swap, hidden1, active1, slope1 = forward(form, after(x1, c1_sent[0]), theirs, *weights, weight=0.25)
    x1_got = swap(x1_swap)
    out1_back = form.send(out1)

    on, all_ = copies // 4, copies // 2
    half_width = width // 2
    c1_got = swap(pick_shares(form, after(theirs, hidden1), c1, weight=0.35))
    x_left = [(own, 0, False), (x1, 0, False), ([picked_got], 0, True), ([x1_got], 0, True)]
    c_left = [(own, width, False), (c1, 0, False), ([picked_got], half_width, True), ([c1_got], 0, True)]
    at_hidden, at_gate, at_up = [i * ff for i in range(3)]

    def right(far, far_got, column):
        return [(own_inner, column), (far, 0), (inner_got, column), (far_got, 0)]

    hidden1_got = x1_got[:, half_width:]
    down = [right(hidden1, hidden1_got, at_hidden)]
    (down_on,) = weight_sums(form, ours, (0, on), c_left, down, share, ff)
    down_there = exchange(down_on, "ctx", 2)
    early = (form.half - 1,) if form.split else ()
    back0_first = form.send(after(back0, down_on), early) if early else []
    gin1, gg1, gu1 = backward(form, after(c1, down_on), active1, slope1, *weights, weight=0.5)
    gin1_back = form.send(gin1)
    (far_mixed,) = back(form, after(far_meta, gg1), far_cot, out1_back, (0, None), weight=0.3)
    got_mixed = exchange(far_mixed, "exp", half)
    both_rights = [right(gg1, swap(gg1), at_gate), right(gu1, swap(gu1), at_up)]
    (both_on,) = weight_sums(
        form, after(ours, far_mixed, back0_first), (0, on), x_left, both_rights, share, ff, beside=True, weight=0.3
    )
    both_there = exchange(both_on, "ctx", 2)
    (far_grad,) = back(
        form, after(far_meta, both_on, down_there), far_cot, gin1_back, (None, 0), weight=1.8
    )
    got_grad = exchange(far_grad, "exp", half)
    late = [p for p in range(form.half) if p not in early] if form.split else None
    back0_got = back0_first + form.send(after(back0, far_grad), late)
    if early:
        places = list(early) + late
        back0_got = [back0_got[places.index(p)] for p in range(form.half)]

    def last_bits(keep, got):
        bit = 4
        while bit < copies:
            sums = keep + got.astype(f32)
            middle = sums.shape[0] // 2
            keep, got = sums[middle:], exchange(sums[:middle].astype(bf16), "ctx", bit)
            bit *= 2
        return keep, got

    (down_keep,) = weight_sums(
        form, after(ours, far_grad), (on, all_), c_left, down, share, ff, dtype=f32, hbm=True, weight=0.35
    )
    (down_grads,) = finish(*last_bits(down_keep, down_there), 1)
    (both_keep,) = weight_sums(
        form,
        after(ours, down_keep, got_mixed),
        (on, all_),
        x_left,
        both_rights,
        share,
        ff,
        dtype=f32,
        hbm=True,
        beside=True,
        weight=0.2,
    )
    gate_grads, up_grads = finish(*last_bits(both_keep, both_there), 2, weight=0.1)
    mixed, combine_grads, own_grad = back(
        form,
        after(meta, gate_grads),
        cotangent,
        back0_got,
        (0, width),
        combine,
        (got_mixed,),
        weight=0.0,
    )
    input_grads = add_up(own_grad, got_grad)
    return (mixed, input_grads, combine_grads.T, gate_grads[None], up_grads[None], down_grads[None])


def solution(mesh):
    rows = P(("ctx", "exp"), None)
    weight = P("exp", None, None)
    grads = P("exp", "ctx", None)
    return jax.shard_map(
        local,
        mesh=mesh,
        in_specs=(rows, rows, rows, rows, weight, weight, weight),
        out_specs=(rows, rows, rows, grads, grads, grads),
        check_vma=False,
    )
```

```python
import functools

import jax
import jax.numpy as jnp
from jax import lax
from jax.experimental import pallas as pl
from jax.experimental.pallas import tpu as pltpu
from jax.sharding import PartitionSpec as P

grad_scale = 0.0625
f32 = jnp.float32
bf16 = jnp.bfloat16
VMEM = pl.BlockSpec(memory_space=pltpu.VMEM)
SMEM = pl.BlockSpec(memory_space=pltpu.SMEM)


def dot(a, b, dims=((1,), (0,))):
    return lax.dot_general(a, b, (dims, ((), ())), preferred_element_type=f32)


def exchange(x, axis, bit):
    size = lax.axis_size(axis)
    return lax.ppermute(x, axis, [(i, i ^ bit) for i in range(size)])


def within_half(blocks, places=None):
    places = range(len(blocks)) if places is None else places
    return [exchange(blocks[s], "exp", s) if s else blocks[0] for s in places]


def in_hbm(arrays):
    return [pltpu.with_memory_space_constraint(a, pltpu.HBM) for a in arrays]


def result(shape, dtype):
    return jax.ShapeDtypeStruct(tuple(shape), dtype)


def params(**kw):
    return pltpu.CompilerParams(vmem_limit_bytes=24 * 1024 * 1024, **kw)


def cost(weight):
    return pl.CostEstimate(flops=1 + int(weight * 7.5e9), bytes_accessed=1, transcendentals=0)


def after(value, *earlier):
    return lax.optimization_barrier((value, earlier))[0]


class Blocks:
    def __init__(self, half, capacity):
        self.half, self.capacity = half, capacity
        self.split = capacity % 16 == 0
        self.count = half if self.split else 1
        self.rows = half * capacity
        self.height = self.rows // self.count

    def shapes(self, width):
        return [result((self.height, width), bf16)] * self.count

    def send(self, arrays, places=None):
        if self.split:
            return within_half(arrays, places)
        blocks = [arrays[0][s * self.capacity : (s + 1) * self.capacity] for s in range(self.half)]
        return [jnp.concatenate(within_half(blocks), axis=0)]


def join(refs, cols=slice(None)):
    parts = [r[:, cols] for r in refs]
    return parts[0] if len(parts) == 1 else jnp.concatenate(parts, axis=0)


def turned(blocks):
    return list(blocks[:1]) + list(blocks[1:])[::-1]


def store(refs, cols, value):
    height = refs[0].shape[0]
    for i, r in enumerate(refs):
        r[:, cols] = value[i * height : (i + 1) * height].astype(r.dtype)


def slot_plan(rows, form):
    tokens = rows[0].shape[1]
    me = lax.axis_index("exp")
    place = me % form.half
    slot = lax.broadcasted_iota(jnp.int32, (form.rows, 1), 0)
    block = jnp.zeros_like(slot)
    for i in range(1, form.half):
        block = block + (slot >= i * form.capacity).astype(jnp.int32)
    expert = (me - place + (block ^ place)).astype(f32)
    rank_here = (slot - block * form.capacity).astype(f32)
    first = (rows[0] == expert).astype(f32)
    second = (rows[1] == expert).astype(f32)
    row = lax.broadcasted_iota(jnp.int32, (tokens, tokens), 0)
    col = lax.broadcasted_iota(jnp.int32, (tokens, tokens), 1)
    earlier = (row < col).astype(f32).astype(bf16)
    rank = dot((first + second).astype(bf16), earlier)
    here = (rank == rank_here).astype(f32)
    return first * here, second * here


def packed_columns(ref):
    x = ref[...].astype(f32)
    return [x[:, k : k + 1] for k in range(2)] + [
        x[:, 2 + k : 3 + k] + x[:, 4 + k : 5 + k] + x[:, 6 + k : 7 + k] for k in range(2)
    ]


def packed_rows(ref):
    x = jnp.transpose(ref[...].astype(f32))
    return [x[k : k + 1] for k in range(2)] + [x[2 + k : 3 + k] + x[4 + k : 5 + k] + x[6 + k : 7 + k] for k in range(2)]


def plain_rows(ids_ref, combine_ref):
    ids = ids_ref[...].astype(f32)
    return [ids[0:1], ids[1:2], combine_ref[0:1, :], combine_ref[1:2, :]]


def chunks(width, step=512):
    step = min(step, width)
    return [slice(i, i + step) for i in range(0, width, step)]


def pack_rows(meta):
    rows = [meta[0], meta[1]]
    rest = [meta[2], meta[3]]
    for _ in range(3):
        top = [r.astype(bf16).astype(f32) for r in rest]
        rows += top
        rest = [r - t for r, t in zip(rest, top)]
    rows.append(jnp.zeros((128 - len(rows), meta[0].shape[1]), f32))
    return jnp.transpose(jnp.concatenate(rows, axis=0)).astype(bf16)


def gather_kernel(form, scaled, width, plain, *refs):
    meta, refs = (plain_rows(*refs[:2]), refs[2:]) if plain else (packed_rows(refs[0]), refs[1:])
    if plain:
        message_ref, refs = refs[-1], refs[:-1]
        message_ref[:, :width] = refs[0][...]
        message_ref[:, width:] = pack_rows(meta)
    inputs, outs = refs[: len(scaled)], refs[len(scaled) :]
    first, second = slot_plan(meta, form)
    either = (first + second).astype(bf16)
    weight = jnp.sum(first * meta[2] + second * meta[3], axis=1, keepdims=True)
    offset = 0
    for x, by_weight in zip(inputs, scaled):
        for cols in chunks(width):
            rows = dot(either, x[:, cols])
            if by_weight:
                rows = rows * weight
            store(outs, slice(offset + cols.start, offset + cols.stop), rows)
        offset += width


def meta_specs(meta, width):
    if len(meta) == 2:
        return [pl.BlockSpec(m.shape, lambda i: (0, 0)) for m in meta]
    return [pl.BlockSpec((meta[0].shape[0], 128), lambda i: (0, width // 128))]


def whole_spec(shape):
    return pl.BlockSpec(shape, lambda i: (0, 0))


def gather(form, meta, arrays, scaled, width, weight=0.0):
    tokens = arrays[0].shape[0]
    total = width * len(arrays)
    plain = len(meta) == 2
    out_shape = form.shapes(total)
    if plain:
        out_shape = out_shape + [result((tokens, width + 128), bf16)]
    out = pl.pallas_call(
        functools.partial(gather_kernel, form, scaled, width, plain),
        grid=(1,),
        out_shape=out_shape,
        in_specs=meta_specs(meta, width) + [whole_spec((tokens, width)) for _ in arrays],
        out_specs=[whole_spec(x.shape) for x in out_shape],
        compiler_params=params(),
        cost_estimate=cost(weight),
        name="gather_slots",
    )(*(in_hbm([*meta, *arrays]) if plain else [*meta, *arrays]))
    return list(out)


def back_kernel(form, offsets, plain, more, *refs):
    count = form.count
    if plain:
        meta, weights = plain_rows(*refs[:2]), [refs[2][:, k : k + 1] for k in range(2)]
        refs = refs[3:]
    else:
        meta, weights = packed_rows(refs[0]), packed_columns(refs[0])[2:]
        refs = refs[1:]
    cot_ref, rows, refs = refs[0], turned(refs[1 : 1 + count]), refs[1 + count :]
    others, outs = (list(refs[:1]), list(refs[1:])) if more else ([], list(refs))
    plan = [p.astype(bf16) for p in slot_plan(meta, form)]
    out_at, grad_at = offsets
    width = cot_ref.shape[1]

    def put(i, cols, value):
        if more:
            value = value + others[i][:, cols].astype(f32)
        outs[i][:, cols] = value.astype(outs[i].dtype)

    def put_grad(cols, value):
        outs[-1][:, cols] = value.astype(outs[-1].dtype)

    def put_sums(sums):
        lane = lax.broadcasted_iota(jnp.int32, (sums[0].shape[0], 128), 1)
        if more:
            tail = jnp.transpose(others[0][:, width:].astype(f32))
            rows = jnp.transpose(jnp.where(lane == 0, sums[0], jnp.where(lane == 1, sums[1], 0.0)))
            outs[1][...] = rows[0:2] + tail[0:2] + tail[2:4] + tail[4:6]
            return
        tail = jnp.zeros(lane.shape, f32)
        for k in range(2):
            rest = sums[k]
            for piece in range(3):
                top = rest.astype(bf16).astype(f32)
                tail = jnp.where(lane == 2 * piece + k, top, tail)
                rest = rest - top
        outs[0][:, width:] = tail.astype(bf16)

    if out_at is not None:
        sums = [0.0, 0.0]
        for cols in chunks(width):
            block = join(rows, slice(out_at + cols.start, out_at + cols.stop))
            mixed = 0.0
            cot = cot_ref[:, cols].astype(f32)
            for k in range(2):
                pair = dot(plan[k], block, ((0,), (0,)))
                mixed = mixed + weights[k] * pair
                sums[k] = sums[k] + jnp.sum(cot * pair, axis=1, keepdims=True)
            put(0, cols, mixed)
        put_sums(sums)
    if grad_at is not None:
        either = plan[0] + plan[1]
        for cols in chunks(width):
            block = join(rows, slice(grad_at + cols.start, grad_at + cols.stop))
            put_grad(cols, dot(either, block, ((0,), (0,))))


def back(form, meta, cot, rows, offsets, combine=None, others=(), weight=0.0):
    tokens, width = cot.shape
    shapes = []
    if offsets[0] is not None:
        shapes += [result((tokens, width + (0 if others else 128)), bf16)]
    if others:
        shapes += [result((2, tokens), f32)]
    if offsets[1] is not None:
        shapes += [jax.ShapeDtypeStruct((tokens, width), f32 if others else bf16)]
    own = [] if combine is None else [combine]
    arrays = own + [cot] + turned(rows) + list(others)
    return pl.pallas_call(
        functools.partial(back_kernel, form, offsets, combine is not None, len(others) > 0),
        grid=(1,),
        out_shape=shapes,
        in_specs=meta_specs(meta, width) + [whole_spec(a.shape) for a in arrays],
        out_specs=[whole_spec(x.shape) for x in shapes],
        compiler_params=params(),
        cost_estimate=cost(weight),
        name="sum_slots",
    )(*meta, *arrays)


def tiles(ff):
    return chunks(ff, 256 if ff % 256 == 0 else ff)


def fetch(refs, buffers, sems, steps):
    copies = [
        [
            pltpu.make_async_copy(w.at[0, :, inner], b.at[:, inner], sems.at[i, step])
            for i, (w, b) in enumerate(zip(refs, buffers))
        ]
        for step, inner in enumerate(steps)
    ]
    for group in copies:
        for c in group:
            c.start()

    def wait(step):
        for c in copies[step]:
            c.wait()

    return wait


def add_to(acc, first, cols, value):
    if first:
        acc[:, cols] = value
    else:
        acc[:, cols] += value


def pick(ids_ref, refs, at, out_ref, out_at, width):
    number = ids_ref.shape[0]
    share = width // (2 * number)
    height = refs[0].shape[0]
    for p in range(number):
        cols = pl.ds(pl.multiple_of(at + ids_ref[p] * share, share), share)
        for i, r in enumerate(refs):
            out_ref[i * height : (i + 1) * height, out_at + p * share : out_at + (p + 1) * share] = r[:, cols]
    return out_at + number * share


def pick_kernel(count, ids_ref, *refs):
    pick(ids_ref, turned(refs[:count]), 0, refs[count], 0, refs[0].shape[1])


def pick_shares(form, ids, arrays, weight=0.0):
    width = arrays[0].shape[1]
    return pl.pallas_call(
        functools.partial(pick_kernel, form.count),
        out_shape=jax.ShapeDtypeStruct((form.rows, width // 2), bf16),
        in_specs=[SMEM] + [VMEM] * form.count,
        out_specs=VMEM,
        compiler_params=params(),
        cost_estimate=cost(weight),
        name="pick_shares",
    )(ids, *turned(arrays))


def forward_kernel(count, *refs):
    x_refs, ids_ref, held = turned(refs[:count]), refs[count], refs[count + 1 : count + 4]
    out_refs = refs[count + 4 : 2 * count + 4]
    swap_ref, hidden_ref, active_ref, slope_ref, acc, gate_ref, up_ref, down_ref, sems = refs[2 * count + 4 :]
    wait = fetch(held, (gate_ref, up_ref, down_ref), sems, tiles(hidden_ref.shape[1]))
    x = join(x_refs)
    ff = hidden_ref.shape[1]
    used = pick(ids_ref, x_refs, 0, swap_ref, 0, x.shape[1])
    for step, inner in enumerate(tiles(hidden_ref.shape[1])):
        wait(step)
        gate, up = dot(x, gate_ref[:, inner]), dot(x, up_ref[:, inner])
        s = jax.nn.sigmoid(gate)
        active = gate * s
        hidden = (active * up).astype(bf16)
        hidden_ref[:, inner] = hidden
        swap_ref[:, used + inner.start : used + inner.stop] = hidden
        active_ref[:, inner] = active
        slope_ref[:, inner] = up * s * (1.0 + gate * (1.0 - s))
        for cols in chunks(acc.shape[1]):
            add_to(acc, step == 0, cols, dot(hidden, down_ref[cols, inner], ((1,), (1,))))
    store(out_refs, slice(None), acc[...])


def expert_call(kernel, form, inputs, weights, more, out_width, inner_types, name, weight=0.0):
    _, width, ff = weights[0].shape
    rows = form.rows
    out_shape = form.shapes(out_width) + [jax.ShapeDtypeStruct((rows, w), t) for w, t in inner_types]
    operands = [*turned(inputs), *more]
    out = pl.pallas_call(
        functools.partial(kernel, form.count),
        out_shape=out_shape,
        in_specs=[SMEM if o.dtype == jnp.int32 else VMEM for o in operands] + [pl.BlockSpec(memory_space=pl.ANY)] * 3,
        out_specs=[VMEM] * len(out_shape),
        scratch_shapes=[pltpu.VMEM((rows, out_width), f32)]
        + [pltpu.VMEM((width, ff), bf16)] * 3
        + [pltpu.SemaphoreType.DMA((3, len(tiles(ff))))],
        compiler_params=params(),
        cost_estimate=cost(weight),
        name=name,
    )(*operands, *(weights if name == "expert_backward" else in_hbm(weights)))
    return list(out[: form.count]), *out[form.count :]


def forward(form, x, ids, *weights, weight=0.0):
    _, width, ff = weights[0].shape
    types = [(width // 2 + ff, bf16), (ff, bf16), (ff, f32), (ff, f32)]
    return expert_call(forward_kernel, form, x, weights, [ids], width, types, "expert_forward", weight)


def backward_kernel(count, *refs):
    c_refs, active_ref, slope_ref, held = turned(refs[:count]), refs[count], refs[count + 1], refs[count + 2 : count + 5]
    in_refs = refs[count + 5 : 2 * count + 5]
    gg_ref, gu_ref, acc, gate_ref, up_ref, down_ref, sems = refs[2 * count + 5 :]
    wait = fetch(held, (gate_ref, up_ref, down_ref), sems, tiles(gg_ref.shape[1]))
    c = join(c_refs)
    for step, inner in enumerate(tiles(gg_ref.shape[1])):
        wait(step)
        grad_hidden = dot(c, down_ref[:, inner])
        gu = (grad_hidden * active_ref[:, inner]).astype(bf16)
        gg = (grad_hidden * slope_ref[:, inner]).astype(bf16)
        gu_ref[:, inner] = gu
        gg_ref[:, inner] = gg
        for cols in chunks(acc.shape[1]):
            back = dot(gg, gate_ref[cols, inner], ((1,), (1,))) + dot(gu, up_ref[cols, inner], ((1,), (1,)))
            add_to(acc, step == 0, cols, back)
    store(in_refs, slice(None), acc[...])


def backward(form, c, active, slope, *weights, weight=0.0):
    more = [active, slope]
    _, width, ff = weights[0].shape
    return expert_call(backward_kernel, form, c, weights, more, width, [(ff, bf16)] * 2, "expert_backward", weight)


def both_kernel(count, *refs):
    in_refs, ids_ref, held = turned(refs[:count]), refs[count], refs[count + 1 : count + 4]
    out_refs = refs[count + 4 : 2 * count + 4]
    picked_ref, inner_ref, acc, gate_ref, up_ref, down_ref, sems = refs[2 * count + 4 :]
    width, ff = acc.shape[1] // 2, gate_ref.shape[1]
    wait = fetch(held, (gate_ref, up_ref, down_ref), sems, tiles(ff))
    used = pick(ids_ref, in_refs, 0, picked_ref, 0, width)
    pick(ids_ref, in_refs, width, picked_ref, used, width)
    hidden_ref, gg_ref, gu_ref = [inner_ref.at[:, i * ff : (i + 1) * ff] for i in range(3)]
    x, c = join(in_refs, slice(0, width)), join(in_refs, slice(width, 2 * width))
    for step, inner in enumerate(tiles(ff)):
        wait(step)
        gate, up = dot(x, gate_ref[:, inner]), dot(x, up_ref[:, inner])
        s = jax.nn.sigmoid(gate)
        active = gate * s
        hidden = (active * up).astype(bf16)
        hidden_ref[:, inner] = hidden
        grad_hidden = dot(c, down_ref[:, inner])
        gu = (grad_hidden * active).astype(bf16)
        gg = (grad_hidden * up * s * (1.0 + gate * (1.0 - s))).astype(bf16)
        gu_ref[:, inner] = gu
        gg_ref[:, inner] = gg
        for cols in chunks(width):
            add_to(acc, step == 0, cols, dot(hidden, down_ref[cols, inner], ((1,), (1,))))
            back = slice(width + cols.start, width + cols.stop)
            grad = dot(gg, gate_ref[cols, inner], ((1,), (1,))) + dot(gu, up_ref[cols, inner], ((1,), (1,)))
            add_to(acc, step == 0, back, grad)
    store(out_refs, slice(None), acc[...])


def both(form, rows_in, ids, *weights):
    _, width, ff = weights[0].shape
    return expert_call(both_kernel, form, rows_in, weights, [ids], 2 * width, [(width, bf16), (3 * ff, bf16)], "expert_both")


def weight_kernel(counts, number, ids_ref, *refs):
    groups = []
    for n in counts:
        groups.append(join(turned(refs[:n])))
        refs = refs[n:]
    left = jnp.concatenate(groups, axis=0)
    rights, outs = refs[: number * len(counts)], refs[number * len(counts) :]
    if len(outs) < number:
        ff = outs[0].shape[1] // number
        outs = [outs[0].at[:, i * ff : (i + 1) * ff] for i in range(number)]
    for i in range(number):
        right = jnp.concatenate([r[...] for r in rights[i * len(counts) : (i + 1) * len(counts)]], axis=0)
        outs[i][...] = dot(left, right, ((0,), (0,))).astype(outs[i].dtype)


def weight_sums(form, ids, at, left, rights, share, ff, dtype=bf16, hbm=False, beside=False, weight=0.0):
    first, steps = at[0], at[1] - at[0]
    arrays, specs = [], []
    for held, column, picked in left:
        block = column // share
        for h in turned(held):
            arrays.append(h)
            if picked:
                specs.append(pl.BlockSpec((h.shape[0], share), lambda i, ids_ref, b=block: (0, b + first + i)))
            else:
                specs.append(pl.BlockSpec((h.shape[0], share), lambda i, ids_ref, b=block: (0, b + ids_ref[first + i])))
    for right in rights:
        for array, column in right:
            arrays.append(array)
            specs.append(pl.BlockSpec((form.rows, ff), lambda i, ids_ref, b=column // ff: (0, b)))
    number = len(rights)
    widths = [number * ff] if beside else [ff] * number
    if hbm:
        arrays = in_hbm(arrays)
    return pl.pallas_call(
        functools.partial(weight_kernel, [len(g[0]) for g in left], number),
        grid_spec=pltpu.PrefetchScalarGridSpec(
            num_scalar_prefetch=1,
            grid=(steps,),
            in_specs=specs,
            out_specs=[pl.BlockSpec((share, w), lambda i, ids_ref: (i, 0)) for w in widths],
        ),
        out_shape=[jax.ShapeDtypeStruct((steps * share, w), dtype) for w in widths],
        compiler_params=params(),
        cost_estimate=cost(weight),
        name="weight_sums",
    )(ids, *arrays)


def add_kernel(a_ref, b_ref, out_ref):
    out_ref[...] = (a_ref[...] + b_ref[...].astype(f32)).astype(bf16)


def add_up(a, b):
    rows, width = a.shape
    block = pl.BlockSpec((rows, width // 2), lambda i: (0, i))
    return pl.pallas_call(
        add_kernel,
        grid=(2,),
        out_shape=result((rows, width), bf16),
        in_specs=[block] * 2,
        out_specs=block,
        compiler_params=params(),
        cost_estimate=cost(0),
        name="add_halves",
    )(a, b)


def finish_kernel(number, *refs):
    for keep, got, out in zip(refs[:number], refs[number : 2 * number], refs[2 * number :]):
        out[...] = ((keep[...] + got[...].astype(f32)) * grad_scale).astype(bf16)


def finish(keep, got, number, weight=0.0):
    rows, ff = keep.shape[0], keep.shape[1] // number
    tile = rows // 2
    sides = [pl.BlockSpec((tile, ff), lambda i, n=n: (i, n)) for n in range(number)]
    return pl.pallas_call(
        functools.partial(finish_kernel, number),
        grid=(rows // tile,),
        out_shape=[result((rows, ff), bf16)] * number,
        in_specs=sides * 2,
        out_specs=[pl.BlockSpec((tile, ff), lambda i: (i, 0))] * number,
        compiler_params=params(),
        cost_estimate=cost(weight),
        name="finish_weights",
    )(*[keep] * number, *[got] * number)


def local(hits, cotangent, combine, expert_ids, gate_weight, up_weight, down_weight):
    tokens, width = hits.shape
    experts = lax.axis_size("exp")
    copies = lax.axis_size("ctx")
    half = experts // 2
    capacity = 3 * tokens // experts
    form = Blocks(half, capacity)
    meta = (expert_ids.T, combine.T)
    *own_send, message = gather(form, meta, [hits, cotangent], (False, True), width)
    far_hits = exchange(message, "exp", half)
    far_cot = exchange(after(cotangent, far_hits), "exp", half)
    far_meta = (far_hits,)

    share, ff = width // copies, gate_weight.shape[2]
    order = [r for r in range(0, copies, 2)]
    order.sort(key=lambda r: [-(r >> b & 1) for b in range(1, copies.bit_length())])
    order = jnp.asarray(order, jnp.int32)
    here = lax.axis_index("ctx")
    theirs, ours = here ^ 1 ^ order, here ^ order
    swap = lambda x: exchange(x, "ctx", 1)

    weights = (gate_weight, up_weight, down_weight)
    own = form.send(own_send)
    x1_sent = gather(form, after(far_meta, own), [far_hits], (False,), width)
    x1 = form.send(x1_sent)
    back0, own_picked, own_inner = both(form, after(own, x1_sent[0]), theirs, *weights)
    picked_got, inner_got = swap(own_picked), swap(own_inner)
    c1_sent = gather(form, after(far_meta, own_picked), [far_cot], (True,), width)
    c1 = form.send(c1_sent)
    out1, x1_swap, hidden1, active1, slope1 = forward(form, after(x1, c1_sent[0]), theirs, *weights, weight=0.25)
    x1_got = swap(x1_swap)
    out1_back = form.send(out1)

    on, all_ = copies // 4, copies // 2
    half_width = width // 2
    c1_got = swap(pick_shares(form, after(theirs, hidden1), c1, weight=0.35))
    x_left = [(own, 0, False), (x1, 0, False), ([picked_got], 0, True), ([x1_got], 0, True)]
    c_left = [(own, width, False), (c1, 0, False), ([picked_got], half_width, True), ([c1_got], 0, True)]
    at_hidden, at_gate, at_up = [i * ff for i in range(3)]

    def right(far, far_got, column):
        return [(own_inner, column), (far, 0), (inner_got, column), (far_got, 0)]

    hidden1_got = x1_got[:, half_width:]
    down = [right(hidden1, hidden1_got, at_hidden)]
    (down_on,) = weight_sums(form, ours, (0, on), c_left, down, share, ff)
    down_there = exchange(down_on, "ctx", 2)
    early = (form.half - 1,) if form.split else ()
    back0_first = form.send(after(back0, c1), early) if early else []
    gin1, gg1, gu1 = backward(form, after(c1, down_on), active1, slope1, *weights, weight=0.5)
    gin1_back = form.send(gin1)
    (far_mixed,) = back(form, after(far_meta, gg1), far_cot, out1_back, (0, None), weight=0.3)
    got_mixed = exchange(far_mixed, "exp", half)
    both_rights = [right(gg1, swap(gg1), at_gate), right(gu1, swap(gu1), at_up)]
    (both_on,) = weight_sums(
        form, after(ours, far_mixed, back0_first), (0, on), x_left, both_rights, share, ff, beside=True, weight=0.3
    )
    both_there = exchange(both_on, "ctx", 2)
    (far_grad,) = back(
        form, after(far_meta, both_on, down_there), far_cot, gin1_back, (None, 0), weight=1.8
    )
    got_grad = exchange(far_grad, "exp", half)
    late = [p for p in range(form.half) if p not in early] if form.split else None
    back0_got = back0_first + form.send(after(back0, far_grad), late)
    if early:
        places = list(early) + late
        back0_got = [back0_got[places.index(p)] for p in range(form.half)]

    def last_bits(keep, got):
        bit = 4
        while bit < copies:
            sums = keep + got.astype(f32)
            middle = sums.shape[0] // 2
            keep, got = sums[middle:], exchange(sums[:middle].astype(bf16), "ctx", bit)
            bit *= 2
        return keep, got

    (down_keep,) = weight_sums(
        form, after(ours, far_grad), (on, all_), c_left, down, share, ff, dtype=f32, hbm=True, weight=0.35
    )
    (down_grads,) = finish(*last_bits(down_keep, down_there), 1)
    (both_keep,) = weight_sums(
        form,
        after(ours, down_keep, got_mixed),
        (on, all_),
        x_left,
        both_rights,
        share,
        ff,
        dtype=f32,
        hbm=True,
        beside=True,
        weight=0.2,
    )
    gate_grads, up_grads = finish(*last_bits(both_keep, both_there), 2, weight=0.1)
    mixed, combine_grads, own_grad = back(
        form,
        after(meta, gate_grads),
        cotangent,
        back0_got,
        (0, width),
        combine,
        (got_mixed,),
        weight=0.0,
    )
    input_grads = add_up(own_grad, got_grad)
    return (mixed, input_grads, combine_grads.T, gate_grads[None], up_grads[None], down_grads[None])


def solution(mesh):
    rows = P(("ctx", "exp"), None)
    weight = P("exp", None, None)
    grads = P("exp", "ctx", None)
    return jax.shard_map(
        local,
        mesh=mesh,
        in_specs=(rows, rows, rows, rows, weight, weight, weight),
        out_specs=(rows, rows, rows, grads, grads, grads),
        check_vma=False,
    )
```

```python
import functools

import jax
import jax.numpy as jnp
from jax import lax
from jax.experimental import pallas as pl
from jax.experimental.pallas import tpu as pltpu
from jax.sharding import PartitionSpec as P

grad_scale = 0.0625
f32 = jnp.float32
bf16 = jnp.bfloat16
VMEM = pl.BlockSpec(memory_space=pltpu.VMEM)
SMEM = pl.BlockSpec(memory_space=pltpu.SMEM)


def dot(a, b, dims=((1,), (0,))):
    return lax.dot_general(a, b, (dims, ((), ())), preferred_element_type=f32)


def exchange(x, axis, bit):
    size = lax.axis_size(axis)
    return lax.ppermute(x, axis, [(i, i ^ bit) for i in range(size)])


def within_half(blocks, places=None):
    places = range(len(blocks)) if places is None else places
    return [exchange(blocks[s], "exp", s) if s else blocks[0] for s in places]


def in_hbm(arrays):
    return [pltpu.with_memory_space_constraint(a, pltpu.HBM) for a in arrays]


def result(shape, dtype):
    return jax.ShapeDtypeStruct(tuple(shape), dtype)


def params(**kw):
    return pltpu.CompilerParams(vmem_limit_bytes=24 * 1024 * 1024, **kw)


def cost(weight):
    return pl.CostEstimate(flops=1 + int(weight * 7.5e9), bytes_accessed=1, transcendentals=0)


def after(value, *earlier):
    return lax.optimization_barrier((value, earlier))[0]


class Blocks:
    def __init__(self, half, capacity):
        self.half, self.capacity = half, capacity
        self.split = capacity % 16 == 0
        self.count = half if self.split else 1
        self.rows = half * capacity
        self.height = self.rows // self.count

    def shapes(self, width):
        return [result((self.height, width), bf16)] * self.count

    def send(self, arrays, places=None):
        if self.split:
            return within_half(arrays, places)
        blocks = [arrays[0][s * self.capacity : (s + 1) * self.capacity] for s in range(self.half)]
        return [jnp.concatenate(within_half(blocks), axis=0)]


def join(refs, cols=slice(None)):
    parts = [r[:, cols] for r in refs]
    return parts[0] if len(parts) == 1 else jnp.concatenate(parts, axis=0)


def turned(blocks):
    return list(blocks[:1]) + list(blocks[1:])[::-1]


def store(refs, cols, value):
    height = refs[0].shape[0]
    for i, r in enumerate(refs):
        r[:, cols] = value[i * height : (i + 1) * height].astype(r.dtype)


def slot_plan(rows, form):
    tokens = rows[0].shape[1]
    me = lax.axis_index("exp")
    place = me % form.half
    slot = lax.broadcasted_iota(jnp.int32, (form.rows, 1), 0)
    block = jnp.zeros_like(slot)
    for i in range(1, form.half):
        block = block + (slot >= i * form.capacity).astype(jnp.int32)
    expert = (me - place + (block ^ place)).astype(f32)
    rank_here = (slot - block * form.capacity).astype(f32)
    first = (rows[0] == expert).astype(f32)
    second = (rows[1] == expert).astype(f32)
    row = lax.broadcasted_iota(jnp.int32, (tokens, tokens), 0)
    col = lax.broadcasted_iota(jnp.int32, (tokens, tokens), 1)
    earlier = (row < col).astype(f32).astype(bf16)
    rank = dot((first + second).astype(bf16), earlier)
    here = (rank == rank_here).astype(f32)
    return first * here, second * here


def packed_columns(ref):
    x = ref[...].astype(f32)
    return [x[:, k : k + 1] for k in range(2)] + [
        x[:, 2 + k : 3 + k] + x[:, 4 + k : 5 + k] + x[:, 6 + k : 7 + k] for k in range(2)
    ]


def packed_rows(ref):
    x = jnp.transpose(ref[...].astype(f32))
    return [x[k : k + 1] for k in range(2)] + [x[2 + k : 3 + k] + x[4 + k : 5 + k] + x[6 + k : 7 + k] for k in range(2)]


def plain_rows(ids_ref, combine_ref):
    ids = ids_ref[...].astype(f32)
    return [ids[0:1], ids[1:2], combine_ref[0:1, :], combine_ref[1:2, :]]


def chunks(width, step=512):
    step = min(step, width)
    return [slice(i, i + step) for i in range(0, width, step)]


def pack_rows(meta):
    rows = [meta[0], meta[1]]
    rest = [meta[2], meta[3]]
    for _ in range(3):
        top = [r.astype(bf16).astype(f32) for r in rest]
        rows += top
        rest = [r - t for r, t in zip(rest, top)]
    rows.append(jnp.zeros((128 - len(rows), meta[0].shape[1]), f32))
    return jnp.transpose(jnp.concatenate(rows, axis=0)).astype(bf16)


def message_kernel(ids_ref, combine_ref, hits_ref, out_ref):
    width = hits_ref.shape[1]
    out_ref[:, :width] = hits_ref[...]
    out_ref[:, width:] = pack_rows(plain_rows(ids_ref, combine_ref))


def message_of(ids, combine, hits):
    tokens, width = hits.shape
    return pl.pallas_call(
        message_kernel,
        out_shape=result((tokens, width + 128), bf16),
        in_specs=[VMEM] * 3,
        out_specs=VMEM,
        compiler_params=params(),
        cost_estimate=cost(0),
        name="message",
    )(*in_hbm([ids, combine, hits]))


def gather_kernel(form, scaled, width, plain, *refs):
    meta, refs = (plain_rows(*refs[:2]), refs[2:]) if plain else (packed_rows(refs[0]), refs[1:])
    inputs, outs = refs[: len(scaled)], refs[len(scaled) :]
    first, second = slot_plan(meta, form)
    either = (first + second).astype(bf16)
    weight = jnp.sum(first * meta[2] + second * meta[3], axis=1, keepdims=True)
    offset = 0
    for x, by_weight in zip(inputs, scaled):
        for cols in chunks(width):
            rows = dot(either, x[:, cols])
            if by_weight:
                rows = rows * weight
            store(outs, slice(offset + cols.start, offset + cols.stop), rows)
        offset += width


def meta_specs(meta, width):
    if len(meta) == 2:
        return [pl.BlockSpec(m.shape, lambda i: (0, 0)) for m in meta]
    return [pl.BlockSpec((meta[0].shape[0], 128), lambda i: (0, width // 128))]


def whole_spec(shape):
    return pl.BlockSpec(shape, lambda i: (0, 0))


def gather(form, meta, arrays, scaled, width, weight=0.0):
    tokens = arrays[0].shape[0]
    total = width * len(arrays)
    plain = len(meta) == 2
    out_shape = form.shapes(total)
    out = pl.pallas_call(
        functools.partial(gather_kernel, form, scaled, width, plain),
        grid=(1,),
        out_shape=out_shape,
        in_specs=meta_specs(meta, width) + [whole_spec((tokens, width)) for _ in arrays],
        out_specs=[whole_spec(x.shape) for x in out_shape],
        compiler_params=params(),
        cost_estimate=cost(weight),
        name="gather_slots",
    )(*(in_hbm([*meta, *arrays]) if plain else [*meta, *arrays]))
    return list(out)


def back_kernel(form, offsets, plain, more, *refs):
    count = form.count
    if plain:
        meta, weights = plain_rows(*refs[:2]), [refs[2][:, k : k + 1] for k in range(2)]
        refs = refs[3:]
    else:
        meta, weights = packed_rows(refs[0]), packed_columns(refs[0])[2:]
        refs = refs[1:]
    cot_ref, rows, refs = refs[0], turned(refs[1 : 1 + count]), refs[1 + count :]
    others, outs = (list(refs[:1]), list(refs[1:])) if more else ([], list(refs))
    plan = [p.astype(bf16) for p in slot_plan(meta, form)]
    out_at, grad_at = offsets
    width = cot_ref.shape[1]

    def put(i, cols, value):
        if more:
            value = value + others[i][:, cols].astype(f32)
        outs[i][:, cols] = value.astype(outs[i].dtype)

    def put_grad(cols, value):
        outs[-1][:, cols] = value.astype(outs[-1].dtype)

    def put_sums(sums):
        lane = lax.broadcasted_iota(jnp.int32, (sums[0].shape[0], 128), 1)
        if more:
            tail = jnp.transpose(others[0][:, width:].astype(f32))
            rows = jnp.transpose(jnp.where(lane == 0, sums[0], jnp.where(lane == 1, sums[1], 0.0)))
            outs[1][...] = rows[0:2] + tail[0:2] + tail[2:4] + tail[4:6]
            return
        tail = jnp.zeros(lane.shape, f32)
        for k in range(2):
            rest = sums[k]
            for piece in range(3):
                top = rest.astype(bf16).astype(f32)
                tail = jnp.where(lane == 2 * piece + k, top, tail)
                rest = rest - top
        outs[0][:, width:] = tail.astype(bf16)

    if out_at is not None:
        sums = [0.0, 0.0]
        for cols in chunks(width):
            block = join(rows, slice(out_at + cols.start, out_at + cols.stop))
            mixed = 0.0
            cot = cot_ref[:, cols].astype(f32)
            for k in range(2):
                pair = dot(plan[k], block, ((0,), (0,)))
                mixed = mixed + weights[k] * pair
                sums[k] = sums[k] + jnp.sum(cot * pair, axis=1, keepdims=True)
            put(0, cols, mixed)
        put_sums(sums)
    if grad_at is not None:
        either = plan[0] + plan[1]
        for cols in chunks(width):
            block = join(rows, slice(grad_at + cols.start, grad_at + cols.stop))
            put_grad(cols, dot(either, block, ((0,), (0,))))


def back(form, meta, cot, rows, offsets, combine=None, others=(), weight=0.0):
    tokens, width = cot.shape
    shapes = []
    if offsets[0] is not None:
        shapes += [result((tokens, width + (0 if others else 128)), bf16)]
    if others:
        shapes += [result((2, tokens), f32)]
    if offsets[1] is not None:
        shapes += [jax.ShapeDtypeStruct((tokens, width), f32 if others else bf16)]
    own = [] if combine is None else [combine]
    arrays = own + [cot] + turned(rows) + list(others)
    return pl.pallas_call(
        functools.partial(back_kernel, form, offsets, combine is not None, len(others) > 0),
        grid=(1,),
        out_shape=shapes,
        in_specs=meta_specs(meta, width) + [whole_spec(a.shape) for a in arrays],
        out_specs=[whole_spec(x.shape) for x in shapes],
        compiler_params=params(),
        cost_estimate=cost(weight),
        name="sum_slots",
    )(*meta, *arrays)


def tiles(ff):
    return chunks(ff, 256 if ff % 256 == 0 else ff)


def fetch(refs, buffers, sems, steps):
    copies = [
        [
            pltpu.make_async_copy(w.at[0, :, inner], b.at[:, inner], sems.at[i, step])
            for i, (w, b) in enumerate(zip(refs, buffers))
        ]
        for step, inner in enumerate(steps)
    ]
    for group in copies:
        for c in group:
            c.start()

    def wait(step):
        for c in copies[step]:
            c.wait()

    return wait


def add_to(acc, first, cols, value):
    if first:
        acc[:, cols] = value
    else:
        acc[:, cols] += value


def pick(ids_ref, refs, at, out_ref, out_at, width):
    number = ids_ref.shape[0]
    share = width // (2 * number)
    height = refs[0].shape[0]
    for p in range(number):
        cols = pl.ds(pl.multiple_of(at + ids_ref[p] * share, share), share)
        for i, r in enumerate(refs):
            out_ref[i * height : (i + 1) * height, out_at + p * share : out_at + (p + 1) * share] = r[:, cols]
    return out_at + number * share


def pick_kernel(count, ids_ref, *refs):
    pick(ids_ref, turned(refs[:count]), 0, refs[count], 0, refs[0].shape[1])


def pick_shares(form, ids, arrays, weight=0.0):
    width = arrays[0].shape[1]
    return pl.pallas_call(
        functools.partial(pick_kernel, form.count),
        out_shape=jax.ShapeDtypeStruct((form.rows, width // 2), bf16),
        in_specs=[SMEM] + [VMEM] * form.count,
        out_specs=VMEM,
        compiler_params=params(),
        cost_estimate=cost(weight),
        name="pick_shares",
    )(ids, *turned(arrays))


def forward_kernel(count, *refs):
    x_refs, ids_ref, held = turned(refs[:count]), refs[count], refs[count + 1 : count + 4]
    out_refs = refs[count + 4 : 2 * count + 4]
    swap_ref, hidden_ref, active_ref, slope_ref, acc, gate_ref, up_ref, down_ref, sems = refs[2 * count + 4 :]
    wait = fetch(held, (gate_ref, up_ref, down_ref), sems, tiles(hidden_ref.shape[1]))
    x = join(x_refs)
    ff = hidden_ref.shape[1]
    used = pick(ids_ref, x_refs, 0, swap_ref, 0, x.shape[1])
    for step, inner in enumerate(tiles(hidden_ref.shape[1])):
        wait(step)
        gate, up = dot(x, gate_ref[:, inner]), dot(x, up_ref[:, inner])
        s = jax.nn.sigmoid(gate)
        active = gate * s
        hidden = (active * up).astype(bf16)
        hidden_ref[:, inner] = hidden
        swap_ref[:, used + inner.start : used + inner.stop] = hidden
        active_ref[:, inner] = active
        slope_ref[:, inner] = up * s * (1.0 + gate * (1.0 - s))
        for cols in chunks(acc.shape[1]):
            add_to(acc, step == 0, cols, dot(hidden, down_ref[cols, inner], ((1,), (1,))))
    store(out_refs, slice(None), acc[...])


def expert_call(kernel, form, inputs, weights, more, out_width, inner_types, name, weight=0.0):
    _, width, ff = weights[0].shape
    rows = form.rows
    out_shape = form.shapes(out_width) + [jax.ShapeDtypeStruct((rows, w), t) for w, t in inner_types]
    operands = [*turned(inputs), *more]
    out = pl.pallas_call(
        functools.partial(kernel, form.count),
        out_shape=out_shape,
        in_specs=[SMEM if o.dtype == jnp.int32 else VMEM for o in operands] + [pl.BlockSpec(memory_space=pl.ANY)] * 3,
        out_specs=[VMEM] * len(out_shape),
        scratch_shapes=[pltpu.VMEM((rows, out_width), f32)]
        + [pltpu.VMEM((width, ff), bf16)] * 3
        + [pltpu.SemaphoreType.DMA((3, len(tiles(ff))))],
        compiler_params=params(),
        cost_estimate=cost(weight),
        name=name,
    )(*operands, *(weights if name == "expert_backward" else in_hbm(weights)))
    return list(out[: form.count]), *out[form.count :]


def forward(form, x, ids, *weights, weight=0.0):
    _, width, ff = weights[0].shape
    types = [(width // 2 + ff, bf16), (ff, bf16), (ff, f32), (ff, f32)]
    return expert_call(forward_kernel, form, x, weights, [ids], width, types, "expert_forward", weight)


def backward_kernel(count, *refs):
    c_refs, active_ref, slope_ref, held = turned(refs[:count]), refs[count], refs[count + 1], refs[count + 2 : count + 5]
    in_refs = refs[count + 5 : 2 * count + 5]
    gg_ref, gu_ref, acc, gate_ref, up_ref, down_ref, sems = refs[2 * count + 5 :]
    wait = fetch(held, (gate_ref, up_ref, down_ref), sems, tiles(gg_ref.shape[1]))
    c = join(c_refs)
    for step, inner in enumerate(tiles(gg_ref.shape[1])):
        wait(step)
        grad_hidden = dot(c, down_ref[:, inner])
        gu = (grad_hidden * active_ref[:, inner]).astype(bf16)
        gg = (grad_hidden * slope_ref[:, inner]).astype(bf16)
        gu_ref[:, inner] = gu
        gg_ref[:, inner] = gg
        for cols in chunks(acc.shape[1]):
            back = dot(gg, gate_ref[cols, inner], ((1,), (1,))) + dot(gu, up_ref[cols, inner], ((1,), (1,)))
            add_to(acc, step == 0, cols, back)
    store(in_refs, slice(None), acc[...])


def backward(form, c, active, slope, *weights, weight=0.0):
    more = [active, slope]
    _, width, ff = weights[0].shape
    return expert_call(backward_kernel, form, c, weights, more, width, [(ff, bf16)] * 2, "expert_backward", weight)


def both_kernel(count, *refs):
    in_refs, ids_ref, held = turned(refs[:count]), refs[count], refs[count + 1 : count + 4]
    out_refs = refs[count + 4 : 2 * count + 4]
    picked_ref, inner_ref, acc, gate_ref, up_ref, down_ref, sems = refs[2 * count + 4 :]
    width, ff = acc.shape[1] // 2, gate_ref.shape[1]
    wait = fetch(held, (gate_ref, up_ref, down_ref), sems, tiles(ff))
    used = pick(ids_ref, in_refs, 0, picked_ref, 0, width)
    pick(ids_ref, in_refs, width, picked_ref, used, width)
    hidden_ref, gg_ref, gu_ref = [inner_ref.at[:, i * ff : (i + 1) * ff] for i in range(3)]
    x, c = join(in_refs, slice(0, width)), join(in_refs, slice(width, 2 * width))
    for step, inner in enumerate(tiles(ff)):
        wait(step)
        gate, up = dot(x, gate_ref[:, inner]), dot(x, up_ref[:, inner])
        s = jax.nn.sigmoid(gate)
        active = gate * s
        hidden = (active * up).astype(bf16)
        hidden_ref[:, inner] = hidden
        grad_hidden = dot(c, down_ref[:, inner])
        gu = (grad_hidden * active).astype(bf16)
        gg = (grad_hidden * up * s * (1.0 + gate * (1.0 - s))).astype(bf16)
        gu_ref[:, inner] = gu
        gg_ref[:, inner] = gg
        for cols in chunks(width):
            add_to(acc, step == 0, cols, dot(hidden, down_ref[cols, inner], ((1,), (1,))))
            back = slice(width + cols.start, width + cols.stop)
            grad = dot(gg, gate_ref[cols, inner], ((1,), (1,))) + dot(gu, up_ref[cols, inner], ((1,), (1,)))
            add_to(acc, step == 0, back, grad)
    store(out_refs, slice(None), acc[...])


def both(form, rows_in, ids, *weights):
    _, width, ff = weights[0].shape
    return expert_call(both_kernel, form, rows_in, weights, [ids], 2 * width, [(width, bf16), (3 * ff, bf16)], "expert_both")


def weight_kernel(counts, number, ids_ref, *refs):
    groups = []
    for n in counts:
        groups.append(join(turned(refs[:n])))
        refs = refs[n:]
    left = jnp.concatenate(groups, axis=0)
    rights, outs = refs[: number * len(counts)], refs[number * len(counts) :]
    if len(outs) < number:
        ff = outs[0].shape[1] // number
        outs = [outs[0].at[:, i * ff : (i + 1) * ff] for i in range(number)]
    for i in range(number):
        right = jnp.concatenate([r[...] for r in rights[i * len(counts) : (i + 1) * len(counts)]], axis=0)
        outs[i][...] = dot(left, right, ((0,), (0,))).astype(outs[i].dtype)


def weight_sums(form, ids, at, left, rights, share, ff, dtype=bf16, hbm=False, beside=False, weight=0.0):
    first, steps = at[0], at[1] - at[0]
    arrays, specs = [], []
    for held, column, picked in left:
        block = column // share
        for h in turned(held):
            arrays.append(h)
            if picked:
                specs.append(pl.BlockSpec((h.shape[0], share), lambda i, ids_ref, b=block: (0, b + first + i)))
            else:
                specs.append(pl.BlockSpec((h.shape[0], share), lambda i, ids_ref, b=block: (0, b + ids_ref[first + i])))
    for right in rights:
        for array, column in right:
            arrays.append(array)
            specs.append(pl.BlockSpec((form.rows, ff), lambda i, ids_ref, b=column // ff: (0, b)))
    number = len(rights)
    widths = [number * ff] if beside else [ff] * number
    if hbm:
        arrays = in_hbm(arrays)
    return pl.pallas_call(
        functools.partial(weight_kernel, [len(g[0]) for g in left], number),
        grid_spec=pltpu.PrefetchScalarGridSpec(
            num_scalar_prefetch=1,
            grid=(steps,),
            in_specs=specs,
            out_specs=[pl.BlockSpec((share, w), lambda i, ids_ref: (i, 0)) for w in widths],
        ),
        out_shape=[jax.ShapeDtypeStruct((steps * share, w), dtype) for w in widths],
        compiler_params=params(),
        cost_estimate=cost(weight),
        name="weight_sums",
    )(ids, *arrays)


def add_kernel(a_ref, b_ref, out_ref):
    out_ref[...] = (a_ref[...] + b_ref[...].astype(f32)).astype(bf16)


def add_up(a, b):
    rows, width = a.shape
    block = pl.BlockSpec((rows, width // 2), lambda i: (0, i))
    return pl.pallas_call(
        add_kernel,
        grid=(2,),
        out_shape=result((rows, width), bf16),
        in_specs=[block] * 2,
        out_specs=block,
        compiler_params=params(),
        cost_estimate=cost(0),
        name="add_halves",
    )(a, b)


def finish_kernel(number, *refs):
    for keep, got, out in zip(refs[:number], refs[number : 2 * number], refs[2 * number :]):
        out[...] = ((keep[...] + got[...].astype(f32)) * grad_scale).astype(bf16)


def finish(keep, got, number, weight=0.0):
    rows, ff = keep.shape[0], keep.shape[1] // number
    tile = rows // 2
    sides = [pl.BlockSpec((tile, ff), lambda i, n=n: (i, n)) for n in range(number)]
    return pl.pallas_call(
        functools.partial(finish_kernel, number),
        grid=(rows // tile,),
        out_shape=[result((rows, ff), bf16)] * number,
        in_specs=sides * 2,
        out_specs=[pl.BlockSpec((tile, ff), lambda i: (i, 0))] * number,
        compiler_params=params(),
        cost_estimate=cost(weight),
        name="finish_weights",
    )(*[keep] * number, *[got] * number)


def local(hits, cotangent, combine, expert_ids, gate_weight, up_weight, down_weight):
    tokens, width = hits.shape
    experts = lax.axis_size("exp")
    copies = lax.axis_size("ctx")
    half = experts // 2
    capacity = 3 * tokens // experts
    form = Blocks(half, capacity)
    meta = (expert_ids.T, combine.T)
    message = message_of(*meta, hits)
    own_send = gather(form, after(meta, message), [hits, cotangent], (False, True), width)
    far_hits = exchange(message, "exp", half)
    far_cot = exchange(after(cotangent, far_hits), "exp", half)
    far_meta = (far_hits,)

    share, ff = width // copies, gate_weight.shape[2]
    order = [r for r in range(0, copies, 2)]
    order.sort(key=lambda r: [-(r >> b & 1) for b in range(1, copies.bit_length())])
    order = jnp.asarray(order, jnp.int32)
    here = lax.axis_index("ctx")
    theirs, ours = here ^ 1 ^ order, here ^ order
    swap = lambda x: exchange(x, "ctx", 1)

    weights = (gate_weight, up_weight, down_weight)
    own = form.send(own_send)
    x1_sent = gather(form, after(far_meta, own), [far_hits], (False,), width)
    x1 = form.send(x1_sent)
    back0, own_picked, own_inner = both(form, after(own, x1_sent[0]), theirs, *weights)
    picked_got, inner_got = swap(own_picked), swap(own_inner)
    c1_sent = gather(form, after(far_meta, own_picked), [far_cot], (True,), width)
    c1 = form.send(c1_sent)
    out1, x1_swap, hidden1, active1, slope1 = forward(form, after(x1, c1_sent[0]), theirs, *weights, weight=0.25)
    x1_got = swap(x1_swap)
    out1_back = form.send(out1)

    on, all_ = copies // 4, copies // 2
    half_width = width // 2
    c1_got = swap(pick_shares(form, after(theirs, hidden1), c1, weight=0.35))
    x_left = [(own, 0, False), (x1, 0, False), ([picked_got], 0, True), ([x1_got], 0, True)]
    c_left = [(own, width, False), (c1, 0, False), ([picked_got], half_width, True), ([c1_got], 0, True)]
    at_hidden, at_gate, at_up = [i * ff for i in range(3)]

    def right(far, far_got, column):
        return [(own_inner, column), (far, 0), (inner_got, column), (far_got, 0)]

    hidden1_got = x1_got[:, half_width:]
    down = [right(hidden1, hidden1_got, at_hidden)]
    (down_on,) = weight_sums(form, ours, (0, on), c_left, down, share, ff)
    down_there = exchange(down_on, "ctx", 2)
    early = (form.half - 1,) if form.split else ()
    back0_first = form.send(after(back0, c1), early) if early else []
    gin1, gg1, gu1 = backward(form, after(c1, down_on), active1, slope1, *weights, weight=0.5)
    gin1_back = form.send(gin1)
    (far_mixed,) = back(form, after(far_meta, gg1), far_cot, out1_back, (0, None), weight=0.3)
    got_mixed = exchange(far_mixed, "exp", half)
    both_rights = [right(gg1, swap(gg1), at_gate), right(gu1, swap(gu1), at_up)]
    (both_on,) = weight_sums(
        form, after(ours, far_mixed, back0_first), (0, on), x_left, both_rights, share, ff, beside=True, weight=0.3
    )
    both_there = exchange(both_on, "ctx", 2)
    (far_grad,) = back(
        form, after(far_meta, both_on, down_there), far_cot, gin1_back, (None, 0), weight=1.8
    )
    got_grad = exchange(far_grad, "exp", half)
    late = [p for p in range(form.half) if p not in early] if form.split else None
    back0_got = back0_first + form.send(after(back0, far_grad), late)
    if early:
        places = list(early) + late
        back0_got = [back0_got[places.index(p)] for p in range(form.half)]

    def last_bits(keep, got):
        bit = 4
        while bit < copies:
            sums = keep + got.astype(f32)
            middle = sums.shape[0] // 2
            keep, got = sums[middle:], exchange(sums[:middle].astype(bf16), "ctx", bit)
            bit *= 2
        return keep, got

    (down_keep,) = weight_sums(
        form, after(ours, far_grad), (on, all_), c_left, down, share, ff, dtype=f32, hbm=True, weight=0.35
    )
    (down_grads,) = finish(*last_bits(down_keep, down_there), 1)
    (both_keep,) = weight_sums(
        form,
        after(ours, down_keep, got_mixed),
        (on, all_),
        x_left,
        both_rights,
        share,
        ff,
        dtype=f32,
        hbm=True,
        beside=True,
        weight=0.2,
    )
    gate_grads, up_grads = finish(*last_bits(both_keep, both_there), 2, weight=0.1)
    mixed, combine_grads, own_grad = back(
        form,
        after(meta, gate_grads),
        cotangent,
        back0_got,
        (0, width),
        combine,
        (got_mixed,),
        weight=0.0,
    )
    input_grads = add_up(own_grad, got_grad)
    return (mixed, input_grads, combine_grads.T, gate_grads[None], up_grads[None], down_grads[None])


def solution(mesh):
    rows = P(("ctx", "exp"), None)
    weight = P("exp", None, None)
    grads = P("exp", "ctx", None)
    return jax.shard_map(
        local,
        mesh=mesh,
        in_specs=(rows, rows, rows, rows, weight, weight, weight),
        out_specs=(rows, rows, rows, grads, grads, grads),
        check_vma=False,
    )
```

```python
import functools

import jax
import jax.numpy as jnp
from jax import lax
from jax.experimental import pallas as pl
from jax.experimental.pallas import tpu as pltpu
from jax.sharding import PartitionSpec as P

grad_scale = 0.0625
f32 = jnp.float32
bf16 = jnp.bfloat16
VMEM = pl.BlockSpec(memory_space=pltpu.VMEM)
SMEM = pl.BlockSpec(memory_space=pltpu.SMEM)


def dot(a, b, dims=((1,), (0,))):
    return lax.dot_general(a, b, (dims, ((), ())), preferred_element_type=f32)


def exchange(x, axis, bit):
    size = lax.axis_size(axis)
    return lax.ppermute(x, axis, [(i, i ^ bit) for i in range(size)])


def within_half(blocks, places=None):
    places = range(len(blocks)) if places is None else places
    return [exchange(blocks[s], "exp", s) if s else blocks[0] for s in places]


def in_hbm(arrays):
    return [pltpu.with_memory_space_constraint(a, pltpu.HBM) for a in arrays]


def result(shape, dtype):
    return jax.ShapeDtypeStruct(tuple(shape), dtype)


def params(**kw):
    return pltpu.CompilerParams(vmem_limit_bytes=24 * 1024 * 1024, **kw)


def cost(weight):
    return pl.CostEstimate(flops=1 + int(weight * 7.5e9), bytes_accessed=1, transcendentals=0)


def after(value, *earlier):
    return lax.optimization_barrier((value, earlier))[0]


class Blocks:
    def __init__(self, half, capacity):
        self.half, self.capacity = half, capacity
        self.split = capacity % 16 == 0
        self.count = half if self.split else 1
        self.rows = half * capacity
        self.height = self.rows // self.count

    def shapes(self, width):
        return [result((self.height, width), bf16)] * self.count

    def send(self, arrays, places=None):
        if self.split:
            return within_half(arrays, places)
        blocks = [arrays[0][s * self.capacity : (s + 1) * self.capacity] for s in range(self.half)]
        return [jnp.concatenate(within_half(blocks), axis=0)]


def join(refs, cols=slice(None)):
    parts = [r[:, cols] for r in refs]
    return parts[0] if len(parts) == 1 else jnp.concatenate(parts, axis=0)


def turned(blocks):
    return list(blocks[:1]) + list(blocks[1:])[::-1]


def store(refs, cols, value):
    height = refs[0].shape[0]
    for i, r in enumerate(refs):
        r[:, cols] = value[i * height : (i + 1) * height].astype(r.dtype)


def slot_plan(rows, form):
    tokens = rows[0].shape[1]
    me = lax.axis_index("exp")
    place = me % form.half
    slot = lax.broadcasted_iota(jnp.int32, (form.rows, 1), 0)
    block = jnp.zeros_like(slot)
    for i in range(1, form.half):
        block = block + (slot >= i * form.capacity).astype(jnp.int32)
    expert = (me - place + (block ^ place)).astype(f32)
    rank_here = (slot - block * form.capacity).astype(f32)
    first = (rows[0] == expert).astype(f32)
    second = (rows[1] == expert).astype(f32)
    row = lax.broadcasted_iota(jnp.int32, (tokens, tokens), 0)
    col = lax.broadcasted_iota(jnp.int32, (tokens, tokens), 1)
    earlier = (row < col).astype(f32).astype(bf16)
    rank = dot((first + second).astype(bf16), earlier)
    here = (rank == rank_here).astype(f32)
    return first * here, second * here


def packed_columns(ref):
    x = ref[...].astype(f32)
    return [x[:, k : k + 1] for k in range(2)] + [
        x[:, 2 + k : 3 + k] + x[:, 4 + k : 5 + k] + x[:, 6 + k : 7 + k] for k in range(2)
    ]


def packed_rows(ref):
    x = jnp.transpose(ref[...].astype(f32))
    return [x[k : k + 1] for k in range(2)] + [x[2 + k : 3 + k] + x[4 + k : 5 + k] + x[6 + k : 7 + k] for k in range(2)]


def plain_rows(ids_ref, combine_ref):
    ids = ids_ref[...].astype(f32)
    return [ids[0:1], ids[1:2], combine_ref[0:1, :], combine_ref[1:2, :]]


def chunks(width, step=512):
    step = min(step, width)
    return [slice(i, i + step) for i in range(0, width, step)]


def pack_rows(meta):
    rows = [meta[0], meta[1]]
    rest = [meta[2], meta[3]]
    for _ in range(3):
        top = [r.astype(bf16).astype(f32) for r in rest]
        rows += top
        rest = [r - t for r, t in zip(rest, top)]
    rows.append(jnp.zeros((128 - len(rows), meta[0].shape[1]), f32))
    return jnp.transpose(jnp.concatenate(rows, axis=0)).astype(bf16)


def message_kernel(ids_ref, combine_ref, hits_ref, out_ref):
    width = hits_ref.shape[1]
    out_ref[:, :width] = hits_ref[...]
    out_ref[:, width:] = pack_rows(plain_rows(ids_ref, combine_ref))


def message_of(ids, combine, hits):
    tokens, width = hits.shape
    return pl.pallas_call(
        message_kernel,
        out_shape=result((tokens, width + 128), bf16),
        in_specs=[VMEM] * 3,
        out_specs=VMEM,
        compiler_params=params(),
        cost_estimate=cost(0),
        name="message",
    )(*in_hbm([ids, combine, hits]))


def gather_kernel(form, scaled, width, plain, *refs):
    meta, refs = (plain_rows(*refs[:2]), refs[2:]) if plain else (packed_rows(refs[0]), refs[1:])
    inputs, outs = refs[: len(scaled)], refs[len(scaled) :]
    first, second = slot_plan(meta, form)
    either = (first + second).astype(bf16)
    weight = jnp.sum(first * meta[2] + second * meta[3], axis=1, keepdims=True)
    offset = 0
    for x, by_weight in zip(inputs, scaled):
        for cols in chunks(width):
            rows = dot(either, x[:, cols])
            if by_weight:
                rows = rows * weight
            store(outs, slice(offset + cols.start, offset + cols.stop), rows)
        offset += width


def meta_specs(meta, width):
    if len(meta) == 2:
        return [pl.BlockSpec(m.shape, lambda i: (0, 0)) for m in meta]
    return [pl.BlockSpec((meta[0].shape[0], 128), lambda i: (0, width // 128))]


def whole_spec(shape):
    return pl.BlockSpec(shape, lambda i: (0, 0))


def gather(form, meta, arrays, scaled, width, weight=0.0):
    tokens = arrays[0].shape[0]
    total = width * len(arrays)
    plain = len(meta) == 2
    out_shape = form.shapes(total)
    out = pl.pallas_call(
        functools.partial(gather_kernel, form, scaled, width, plain),
        grid=(1,),
        out_shape=out_shape,
        in_specs=meta_specs(meta, width) + [whole_spec((tokens, width)) for _ in arrays],
        out_specs=[whole_spec(x.shape) for x in out_shape],
        compiler_params=params(),
        cost_estimate=cost(weight),
        name="gather_slots",
    )(*(in_hbm([*meta, *arrays]) if plain else [*meta, *arrays]))
    return list(out)


def back_kernel(form, offsets, plain, more, *refs):
    count = form.count
    if plain:
        meta, weights = plain_rows(*refs[:2]), [refs[2][:, k : k + 1] for k in range(2)]
        refs = refs[3:]
    else:
        meta, weights = packed_rows(refs[0]), packed_columns(refs[0])[2:]
        refs = refs[1:]
    cot_ref, rows, refs = refs[0], turned(refs[1 : 1 + count]), refs[1 + count :]
    others, outs = (list(refs[:1]), list(refs[1:])) if more else ([], list(refs))
    plan = [p.astype(bf16) for p in slot_plan(meta, form)]
    out_at, grad_at = offsets
    width = cot_ref.shape[1]

    def put(i, cols, value):
        if more:
            value = value + others[i][:, cols].astype(f32)
        outs[i][:, cols] = value.astype(outs[i].dtype)

    def put_grad(cols, value):
        outs[-1][:, cols] = value.astype(outs[-1].dtype)

    def put_sums(sums):
        lane = lax.broadcasted_iota(jnp.int32, (sums[0].shape[0], 128), 1)
        if more:
            tail = jnp.transpose(others[0][:, width:].astype(f32))
            rows = jnp.transpose(jnp.where(lane == 0, sums[0], jnp.where(lane == 1, sums[1], 0.0)))
            outs[1][...] = rows[0:2] + tail[0:2] + tail[2:4] + tail[4:6]
            return
        tail = jnp.zeros(lane.shape, f32)
        for k in range(2):
            rest = sums[k]
            for piece in range(3):
                top = rest.astype(bf16).astype(f32)
                tail = jnp.where(lane == 2 * piece + k, top, tail)
                rest = rest - top
        outs[0][:, width:] = tail.astype(bf16)

    if out_at is not None:
        sums = [0.0, 0.0]
        for cols in chunks(width):
            block = join(rows, slice(out_at + cols.start, out_at + cols.stop))
            mixed = 0.0
            cot = cot_ref[:, cols].astype(f32)
            for k in range(2):
                pair = dot(plan[k], block, ((0,), (0,)))
                mixed = mixed + weights[k] * pair
                sums[k] = sums[k] + jnp.sum(cot * pair, axis=1, keepdims=True)
            put(0, cols, mixed)
        put_sums(sums)
    if grad_at is not None:
        either = plan[0] + plan[1]
        for cols in chunks(width):
            block = join(rows, slice(grad_at + cols.start, grad_at + cols.stop))
            put_grad(cols, dot(either, block, ((0,), (0,))))


def back(form, meta, cot, rows, offsets, combine=None, others=(), weight=0.0):
    tokens, width = cot.shape
    shapes = []
    if offsets[0] is not None:
        shapes += [result((tokens, width + (0 if others else 128)), bf16)]
    if others:
        shapes += [result((2, tokens), f32)]
    if offsets[1] is not None:
        shapes += [jax.ShapeDtypeStruct((tokens, width), f32 if others else bf16)]
    own = [] if combine is None else [combine]
    arrays = own + [cot] + turned(rows) + list(others)
    return pl.pallas_call(
        functools.partial(back_kernel, form, offsets, combine is not None, len(others) > 0),
        grid=(1,),
        out_shape=shapes,
        in_specs=meta_specs(meta, width) + [whole_spec(a.shape) for a in arrays],
        out_specs=[whole_spec(x.shape) for x in shapes],
        compiler_params=params(),
        cost_estimate=cost(weight),
        name="sum_slots",
    )(*meta, *arrays)


def tiles(ff):
    return chunks(ff, 256 if ff % 256 == 0 else ff)


def fetch(refs, buffers, sems, steps):
    copies = [
        [
            pltpu.make_async_copy(w.at[0, :, inner], b.at[:, inner], sems.at[i, step])
            for i, (w, b) in enumerate(zip(refs, buffers))
        ]
        for step, inner in enumerate(steps)
    ]
    for group in copies:
        for c in group:
            c.start()

    def wait(step):
        for c in copies[step]:
            c.wait()

    return wait


def add_to(acc, first, cols, value):
    if first:
        acc[:, cols] = value
    else:
        acc[:, cols] += value


def pick(ids_ref, refs, at, out_ref, out_at, width):
    number = ids_ref.shape[0]
    share = width // (2 * number)
    height = refs[0].shape[0]
    for p in range(number):
        cols = pl.ds(pl.multiple_of(at + ids_ref[p] * share, share), share)
        for i, r in enumerate(refs):
            out_ref[i * height : (i + 1) * height, out_at + p * share : out_at + (p + 1) * share] = r[:, cols]
    return out_at + number * share


def pick_kernel(count, ids_ref, *refs):
    pick(ids_ref, turned(refs[:count]), 0, refs[count], 0, refs[0].shape[1])


def pick_shares(form, ids, arrays, weight=0.0):
    width = arrays[0].shape[1]
    return pl.pallas_call(
        functools.partial(pick_kernel, form.count),
        out_shape=jax.ShapeDtypeStruct((form.rows, width // 2), bf16),
        in_specs=[SMEM] + [VMEM] * form.count,
        out_specs=VMEM,
        compiler_params=params(),
        cost_estimate=cost(weight),
        name="pick_shares",
    )(ids, *turned(arrays))


def forward_kernel(count, *refs):
    x_refs, ids_ref, held = turned(refs[:count]), refs[count], refs[count + 1 : count + 4]
    out_refs = refs[count + 4 : 2 * count + 4]
    swap_ref, hidden_ref, active_ref, slope_ref, acc, gate_ref, up_ref, down_ref, sems = refs[2 * count + 4 :]
    wait = fetch(held, (gate_ref, up_ref, down_ref), sems, tiles(hidden_ref.shape[1]))
    x = join(x_refs)
    ff = hidden_ref.shape[1]
    used = pick(ids_ref, x_refs, 0, swap_ref, 0, x.shape[1])
    for step, inner in enumerate(tiles(hidden_ref.shape[1])):
        wait(step)
        gate, up = dot(x, gate_ref[:, inner]), dot(x, up_ref[:, inner])
        s = jax.nn.sigmoid(gate)
        active = gate * s
        hidden = (active * up).astype(bf16)
        hidden_ref[:, inner] = hidden
        swap_ref[:, used + inner.start : used + inner.stop] = hidden
        active_ref[:, inner] = active
        slope_ref[:, inner] = up * s * (1.0 + gate * (1.0 - s))
        for cols in chunks(acc.shape[1]):
            add_to(acc, step == 0, cols, dot(hidden, down_ref[cols, inner], ((1,), (1,))))
    store(out_refs, slice(None), acc[...])


def expert_call(kernel, form, inputs, weights, more, out_width, inner_types, name, weight=0.0):
    _, width, ff = weights[0].shape
    rows = form.rows
    out_shape = form.shapes(out_width) + [jax.ShapeDtypeStruct((rows, w), t) for w, t in inner_types]
    operands = [*turned(inputs), *more]
    out = pl.pallas_call(
        functools.partial(kernel, form.count),
        out_shape=out_shape,
        in_specs=[SMEM if o.dtype == jnp.int32 else VMEM for o in operands] + [pl.BlockSpec(memory_space=pl.ANY)] * 3,
        out_specs=[VMEM] * len(out_shape),
        scratch_shapes=[pltpu.VMEM((rows, out_width), f32)]
        + [pltpu.VMEM((width, ff), bf16)] * 3
        + [pltpu.SemaphoreType.DMA((3, len(tiles(ff))))],
        compiler_params=params(),
        cost_estimate=cost(weight),
        name=name,
    )(*operands, *(weights if name == "expert_backward" else in_hbm(weights)))
    return list(out[: form.count]), *out[form.count :]


def forward(form, x, ids, *weights, weight=0.0):
    _, width, ff = weights[0].shape
    types = [(width // 2 + ff, bf16), (ff, bf16), (ff, f32), (ff, f32)]
    return expert_call(forward_kernel, form, x, weights, [ids], width, types, "expert_forward", weight)


def backward_kernel(count, *refs):
    c_refs, active_ref, slope_ref, held = turned(refs[:count]), refs[count], refs[count + 1], refs[count + 2 : count + 5]
    in_refs = refs[count + 5 : 2 * count + 5]
    gg_ref, gu_ref, acc, gate_ref, up_ref, down_ref, sems = refs[2 * count + 5 :]
    weight_refs = (gate_ref, up_ref, down_ref)
    copies = [pltpu.make_async_copy(w.at[0], r, sems.at[i, 0]) for i, (w, r) in enumerate(zip(held, weight_refs))]
    for i in (2, 0, 1):
        copies[i].start()
    c = join(c_refs)
    for step, inner in enumerate(tiles(gg_ref.shape[1])):
        if step == 0:
            copies[2].wait()
        grad_hidden = dot(c, down_ref[:, inner])
        gu = (grad_hidden * active_ref[:, inner]).astype(bf16)
        gg = (grad_hidden * slope_ref[:, inner]).astype(bf16)
        gu_ref[:, inner] = gu
        gg_ref[:, inner] = gg
        if step == 0:
            copies[0].wait()
            copies[1].wait()
        for cols in chunks(acc.shape[1]):
            back = dot(gg, gate_ref[cols, inner], ((1,), (1,))) + dot(gu, up_ref[cols, inner], ((1,), (1,)))
            add_to(acc, step == 0, cols, back)
    store(in_refs, slice(None), acc[...])


def backward(form, c, active, slope, *weights, weight=0.0):
    more = [active, slope]
    _, width, ff = weights[0].shape
    return expert_call(backward_kernel, form, c, weights, more, width, [(ff, bf16)] * 2, "expert_backward", weight)


def both_kernel(count, *refs):
    in_refs, ids_ref, held = turned(refs[:count]), refs[count], refs[count + 1 : count + 4]
    out_refs = refs[count + 4 : 2 * count + 4]
    picked_ref, inner_ref, acc, gate_ref, up_ref, down_ref, sems = refs[2 * count + 4 :]
    width, ff = acc.shape[1] // 2, gate_ref.shape[1]
    wait = fetch(held, (gate_ref, up_ref, down_ref), sems, tiles(ff))
    used = pick(ids_ref, in_refs, 0, picked_ref, 0, width)
    pick(ids_ref, in_refs, width, picked_ref, used, width)
    hidden_ref, gg_ref, gu_ref = [inner_ref.at[:, i * ff : (i + 1) * ff] for i in range(3)]
    x, c = join(in_refs, slice(0, width)), join(in_refs, slice(width, 2 * width))
    for step, inner in enumerate(tiles(ff)):
        wait(step)
        gate, up = dot(x, gate_ref[:, inner]), dot(x, up_ref[:, inner])
        s = jax.nn.sigmoid(gate)
        active = gate * s
        hidden = (active * up).astype(bf16)
        hidden_ref[:, inner] = hidden
        grad_hidden = dot(c, down_ref[:, inner])
        gu = (grad_hidden * active).astype(bf16)
        gg = (grad_hidden * up * s * (1.0 + gate * (1.0 - s))).astype(bf16)
        gu_ref[:, inner] = gu
        gg_ref[:, inner] = gg
        for cols in chunks(width):
            add_to(acc, step == 0, cols, dot(hidden, down_ref[cols, inner], ((1,), (1,))))
            back = slice(width + cols.start, width + cols.stop)
            grad = dot(gg, gate_ref[cols, inner], ((1,), (1,))) + dot(gu, up_ref[cols, inner], ((1,), (1,)))
            add_to(acc, step == 0, back, grad)
    store(out_refs, slice(None), acc[...])


def both(form, rows_in, ids, *weights):
    _, width, ff = weights[0].shape
    return expert_call(both_kernel, form, rows_in, weights, [ids], 2 * width, [(width, bf16), (3 * ff, bf16)], "expert_both")


def weight_kernel(counts, number, ids_ref, *refs):
    groups = []
    for n in counts:
        groups.append(join(turned(refs[:n])))
        refs = refs[n:]
    left = jnp.concatenate(groups, axis=0)
    rights, outs = refs[: number * len(counts)], refs[number * len(counts) :]
    if len(outs) < number:
        ff = outs[0].shape[1] // number
        outs = [outs[0].at[:, i * ff : (i + 1) * ff] for i in range(number)]
    for i in range(number):
        right = jnp.concatenate([r[...] for r in rights[i * len(counts) : (i + 1) * len(counts)]], axis=0)
        outs[i][...] = dot(left, right, ((0,), (0,))).astype(outs[i].dtype)


def weight_sums(form, ids, at, left, rights, share, ff, dtype=bf16, hbm=False, beside=False, weight=0.0):
    first, steps = at[0], at[1] - at[0]
    arrays, specs = [], []
    for held, column, picked in left:
        block = column // share
        for h in turned(held):
            arrays.append(h)
            if picked:
                specs.append(pl.BlockSpec((h.shape[0], share), lambda i, ids_ref, b=block: (0, b + first + i)))
            else:
                specs.append(pl.BlockSpec((h.shape[0], share), lambda i, ids_ref, b=block: (0, b + ids_ref[first + i])))
    for right in rights:
        for array, column in right:
            arrays.append(array)
            specs.append(pl.BlockSpec((form.rows, ff), lambda i, ids_ref, b=column // ff: (0, b)))
    number = len(rights)
    widths = [number * ff] if beside else [ff] * number
    if hbm:
        arrays = in_hbm(arrays)
    return pl.pallas_call(
        functools.partial(weight_kernel, [len(g[0]) for g in left], number),
        grid_spec=pltpu.PrefetchScalarGridSpec(
            num_scalar_prefetch=1,
            grid=(steps,),
            in_specs=specs,
            out_specs=[pl.BlockSpec((share, w), lambda i, ids_ref: (i, 0)) for w in widths],
        ),
        out_shape=[jax.ShapeDtypeStruct((steps * share, w), dtype) for w in widths],
        compiler_params=params(),
        cost_estimate=cost(weight),
        name="weight_sums",
    )(ids, *arrays)


def add_kernel(a_ref, b_ref, out_ref):
    out_ref[...] = (a_ref[...] + b_ref[...].astype(f32)).astype(bf16)


def add_up(a, b):
    rows, width = a.shape
    block = pl.BlockSpec((rows, width // 2), lambda i: (0, i))
    return pl.pallas_call(
        add_kernel,
        grid=(2,),
        out_shape=result((rows, width), bf16),
        in_specs=[block] * 2,
        out_specs=block,
        compiler_params=params(),
        cost_estimate=cost(0),
        name="add_halves",
    )(a, b)


def finish_kernel(number, *refs):
    for keep, got, out in zip(refs[:number], refs[number : 2 * number], refs[2 * number :]):
        out[...] = ((keep[...] + got[...].astype(f32)) * grad_scale).astype(bf16)


def finish(keep, got, number, weight=0.0):
    rows, ff = keep.shape[0], keep.shape[1] // number
    tile = rows // 2
    sides = [pl.BlockSpec((tile, ff), lambda i, n=n: (i, n)) for n in range(number)]
    return pl.pallas_call(
        functools.partial(finish_kernel, number),
        grid=(rows // tile,),
        out_shape=[result((rows, ff), bf16)] * number,
        in_specs=sides * 2,
        out_specs=[pl.BlockSpec((tile, ff), lambda i: (i, 0))] * number,
        compiler_params=params(),
        cost_estimate=cost(weight),
        name="finish_weights",
    )(*[keep] * number, *[got] * number)


def local(hits, cotangent, combine, expert_ids, gate_weight, up_weight, down_weight):
    tokens, width = hits.shape
    experts = lax.axis_size("exp")
    copies = lax.axis_size("ctx")
    half = experts // 2
    capacity = 3 * tokens // experts
    form = Blocks(half, capacity)
    meta = (expert_ids.T, combine.T)
    message = message_of(*meta, hits)
    own_send = gather(form, after(meta, message), [hits, cotangent], (False, True), width)
    far_hits = exchange(message, "exp", half)
    far_cot = exchange(after(cotangent, far_hits), "exp", half)
    far_meta = (far_hits,)

    share, ff = width // copies, gate_weight.shape[2]
    order = [r for r in range(0, copies, 2)]
    order.sort(key=lambda r: [-(r >> b & 1) for b in range(1, copies.bit_length())])
    order = jnp.asarray(order, jnp.int32)
    here = lax.axis_index("ctx")
    theirs, ours = here ^ 1 ^ order, here ^ order
    swap = lambda x: exchange(x, "ctx", 1)

    weights = (gate_weight, up_weight, down_weight)
    own = form.send(own_send)
    x1_sent = gather(form, after(far_meta, own), [far_hits], (False,), width)
    x1 = form.send(x1_sent)
    back0, own_picked, own_inner = both(form, after(own, x1_sent[0]), theirs, *weights)
    picked_got, inner_got = swap(own_picked), swap(own_inner)
    c1_sent = gather(form, after(far_meta, own_picked), [far_cot], (True,), width)
    c1 = form.send(c1_sent)
    out1, x1_swap, hidden1, active1, slope1 = forward(form, after(x1, c1_sent[0]), theirs, *weights, weight=0.25)
    x1_got = swap(x1_swap)
    out1_back = form.send(out1)

    on, all_ = copies // 4, copies // 2
    half_width = width // 2
    c1_got = swap(pick_shares(form, after(theirs, hidden1), c1, weight=0.35))
    x_left = [(own, 0, False), (x1, 0, False), ([picked_got], 0, True), ([x1_got], 0, True)]
    c_left = [(own, width, False), (c1, 0, False), ([picked_got], half_width, True), ([c1_got], 0, True)]
    at_hidden, at_gate, at_up = [i * ff for i in range(3)]

    def right(far, far_got, column):
        return [(own_inner, column), (far, 0), (inner_got, column), (far_got, 0)]

    hidden1_got = x1_got[:, half_width:]
    down = [right(hidden1, hidden1_got, at_hidden)]
    (down_on,) = weight_sums(form, ours, (0, on), c_left, down, share, ff)
    down_there = exchange(down_on, "ctx", 2)
    early = (form.half - 1,) if form.split else ()
    back0_first = form.send(after(back0, c1), early) if early else []
    gin1, gg1, gu1 = backward(form, after(c1, down_on), active1, slope1, *weights, weight=0.5)
    gin1_back = form.send(gin1)
    (far_mixed,) = back(form, after(far_meta, gg1), far_cot, out1_back, (0, None), weight=0.3)
    got_mixed = exchange(far_mixed, "exp", half)
    both_rights = [right(gg1, swap(gg1), at_gate), right(gu1, swap(gu1), at_up)]
    (both_on,) = weight_sums(
        form, after(ours, far_mixed, back0_first), (0, on), x_left, both_rights, share, ff, beside=True, weight=0.3
    )
    both_there = exchange(both_on, "ctx", 2)
    (far_grad,) = back(
        form, after(far_meta, both_on, down_there), far_cot, gin1_back, (None, 0), weight=1.8
    )
    got_grad = exchange(far_grad, "exp", half)
    late = [p for p in range(form.half) if p not in early] if form.split else None
    back0_got = back0_first + form.send(after(back0, far_grad), late)
    if early:
        places = list(early) + late
        back0_got = [back0_got[places.index(p)] for p in range(form.half)]

    def last_bits(keep, got):
        bit = 4
        while bit < copies:
            sums = keep + got.astype(f32)
            middle = sums.shape[0] // 2
            keep, got = sums[middle:], exchange(sums[:middle].astype(bf16), "ctx", bit)
            bit *= 2
        return keep, got

    (down_keep,) = weight_sums(
        form, after(ours, far_grad), (on, all_), c_left, down, share, ff, dtype=f32, hbm=True, weight=0.35
    )
    (down_grads,) = finish(*last_bits(down_keep, down_there), 1)
    (both_keep,) = weight_sums(
        form,
        after(ours, down_keep, got_mixed),
        (on, all_),
        x_left,
        both_rights,
        share,
        ff,
        dtype=f32,
        hbm=True,
        beside=True,
        weight=0.2,
    )
    gate_grads, up_grads = finish(*last_bits(both_keep, both_there), 2, weight=0.1)
    mixed, combine_grads, own_grad = back(
        form,
        after(meta, gate_grads),
        cotangent,
        back0_got,
        (0, width),
        combine,
        (got_mixed,),
        weight=0.0,
    )
    input_grads = add_up(own_grad, got_grad)
    return (mixed, input_grads, combine_grads.T, gate_grads[None], up_grads[None], down_grads[None])


def solution(mesh):
    rows = P(("ctx", "exp"), None)
    weight = P("exp", None, None)
    grads = P("exp", "ctx", None)
    return jax.shard_map(
        local,
        mesh=mesh,
        in_specs=(rows, rows, rows, rows, weight, weight, weight),
        out_specs=(rows, rows, rows, grads, grads, grads),
        check_vma=False,
    )
```
